32 devices in a mesh: chan: 4 (over x, core), fam: 8 (over z, y).
Axes of the slice: x: 2, y: 2, z: 4, core: 2. Of those that a mesh axis runs over, the one named last changes fastest.
Arguments:
- waveforms: bfloat16 [1024, 256, 256], P('fam', 'chan'), may hold values from -18 to 18
- family_of: int32 [1024], P('fam'), may hold values from 0 to 7, as said below
- channel_mask: int32 [8, 256], P('fam', 'chan'), may hold values 0 or 1
Outputs:
- correlation: float32 [8, 128, 65, 128], P('fam', 'chan')
The draws below stay inside these ranges and needn't reach their ends.
Inputs may be any that keep to these rules, and one draw needn't show every extreme that they name: `family_of`: in each aligned block of 128 events (the events of one index of fam) at most 16 events share a family, and some family has exactly 16 of them.
All inputs are finite; a program needn't handle non-finite values. No bound on the sum of `channel_mask` on one device may be relied on, other than what follows from the above.
Results may differ from the reference program's by a relative error of at most 0.0003.
Values may be sent and summed in bfloat16 or wider, within the bound.
No kernel may reach another device: no remote copies, remote signals or barrier semaphores. Data moves between devices by JAX's collectives and lax.ppermute only.
A program may use at most 192 MiB of HBM per device.

```python
import math
import jax
import jax.numpy as jnp
from jax import lax

SAMPLES = 256
BINS = 128
CHANNELS = 256
MAXLAG = 32
LAGS = 65
SHIFT = 12
EV_DEV = 128
CAP = 16
EVENTS = 1024
FAMS = 8
SLOTS = 128
N_CHAN = 4


def family_ids(key):
    base = jax.random.fold_in(key, 501)
    keys = jax.random.split(base, EVENTS // EV_DEV)

    def one_block(block_key):
        pick, order, place = jax.random.split(block_key, 3)
        hot = jax.random.randint(pick, (), 0, FAMS)
        owner = jnp.arange(FAMS * CAP, dtype=jnp.int32) // CAP
        scores = jax.random.permutation(order, FAMS * CAP).astype(jnp.int32) + (owner != hot).astype(jnp.int32) * (FAMS * CAP)
        chosen = owner[jnp.argsort(scores)][:EV_DEV]
        return chosen[jax.random.permutation(place, EV_DEV)]
    return jax.vmap(one_block)(keys).reshape(-1).astype(jnp.int32)


def draw_family_of(key, part):
    return family_ids(key)


def draw_waveforms(key, part):
    family = family_ids(key)
    key = jax.random.fold_in(key, 3)
    key_shape, key_gain, key_shift, key_noise = jax.random.split(key, 4)
    template = jax.random.truncated_normal(key_shape, -6.0, 6.0, (FAMS, CHANNELS, SAMPLES), jnp.float32)
    gains = jnp.exp(jax.random.uniform(key_gain, (FAMS, CHANNELS), jnp.float32, math.log(0.05), math.log(5.0)))
    offsets = jax.random.randint(key_shift, (EVENTS,), -SHIFT, SHIFT + 1)
    times = (jnp.arange(SAMPLES, dtype=jnp.int32)[None, :] - offsets[:, None]) % SAMPLES
    source = template[family]
    shifted = jnp.take_along_axis(source, jnp.broadcast_to(times[:, None, :], source.shape), axis=2)
    noise = jax.random.truncated_normal(key_noise, -6.0, 6.0, (EVENTS, CHANNELS, SAMPLES), jnp.float32)
    return (0.5 * (gains[family][:, :, None] * shifted + noise)).astype(jnp.bfloat16)


def place_ends(entries, own_key, least, high):
    longest = entries.shape.index(max(entries.shape))
    spots = []
    for shift in (0, 1):
        where = [jax.random.randint(jax.random.fold_in(own_key, axis), (), 0, length) for axis, length in enumerate(entries.shape)]
        where[longest] = (where[longest] + shift) % entries.shape[longest]
        spots.append(tuple(where))
    return entries.at[spots[0]].set(least).at[spots[1]].set(high)


def setup_inputs(seed: int = 0) -> dict:
    key_list = jax.random.split(jax.random.key(seed), 4)
    return {
        "waveforms": draw_waveforms(jax.random.fold_in(key_list[3], 71), 0),
        "family_of": draw_family_of(jax.random.fold_in(key_list[3], 71), 0),
        "channel_mask": place_ends((jax.random.randint(key_list[2], (FAMS, CHANNELS), 0, 8) < 7).astype(jnp.int32), jax.random.fold_in(key_list[2], 1), 0, 1),
    }


HIGH = lax.Precision.HIGHEST

def transform_table(length):
    bins = length // 2
    times = jnp.arange(length, dtype=jnp.int32)
    freqs = jnp.arange(bins, dtype=jnp.int32)
    phase = times[:, None] * freqs[None, :] % length
    angle = phase.astype(jnp.float32) * (2.0 * math.pi / length)
    return jnp.concatenate([jnp.cos(angle), -jnp.sin(angle)], axis=1)

def smoothing_table(bins):
    index = jnp.arange(bins, dtype=jnp.int32)
    near = (jnp.abs(index[:, None] - index[None, :]) <= 4).astype(jnp.float32)
    return near / lax.optimization_barrier(jnp.sum(near, axis=0, keepdims=True))

def lag_table(bins, maxlag, length):
    freqs = jnp.arange(bins, dtype=jnp.int32)
    shifts = jnp.arange(2 * maxlag + 1, dtype=jnp.int32) - maxlag
    phase = shifts[:, None] * freqs[None, :] % length
    angle = phase.astype(jnp.float32) * (2.0 * math.pi / length)
    return jnp.concatenate([jnp.cos(angle), -jnp.sin(angle)], axis=1)

def whiten(windows):
    length = windows.shape[-1]
    bins = length // 2
    flat = windows.reshape(-1, length).astype(jnp.float32)
    spec = jnp.dot(flat, transform_table(length), precision=HIGH, preferred_element_type=jnp.float32)
    real = spec[:, :bins]
    imag = spec[:, bins:]
    power = real * real + imag * imag
    smooth = jnp.dot(power, smoothing_table(bins), precision=HIGH, preferred_element_type=jnp.float32)
    level = lax.optimization_barrier(jnp.mean(power, axis=1, keepdims=True))
    scale = jnp.sqrt(smooth + 0.1 * level + 1e-05)
    white = spec / jnp.concatenate([scale, scale], axis=1)
    return white.reshape(windows.shape[:-1] + (length,))

def paired_columns(cols):
    bins = cols.shape[-1] // 2
    right = cols.reshape(cols.shape[0], cols.shape[1], 2, bins)
    swapped = jnp.stack([-right[:, :, 1], right[:, :, 0]], axis=2)
    return jnp.stack([right, swapped], axis=2)

def pair_terms(rows, both, table):
    bins = rows.shape[-1] // 2
    left = rows.reshape(rows.shape[0], rows.shape[1], 2, bins)
    cross = jnp.einsum('icpk,jcqpk->iqkj', left, both, precision=HIGH)
    cross = cross.reshape(rows.shape[0], 2 * bins, both.shape[0])
    return jnp.einsum('tq,iqj->itj', table, cross, precision=HIGH)

def reference(waveforms, family_of, channel_mask):
    white = whiten(waveforms)
    blocks = family_of.reshape(FAMS, EV_DEV)
    flags = (blocks[:, :, None] == jnp.arange(FAMS, dtype=jnp.int32)[None, None, :]).astype(jnp.int32)
    rank = lax.optimization_barrier(jnp.sum(jnp.cumsum(flags, axis=1) * flags, axis=2)) - 1
    slot = jnp.arange(FAMS, dtype=jnp.int32)[:, None] * CAP + rank
    target = (blocks * SLOTS + slot).reshape(-1).astype(jnp.int32)
    members = jnp.full((FAMS * SLOTS,), EVENTS, jnp.int32).at[target].set(jnp.arange(EVENTS, dtype=jnp.int32))
    padded = jnp.concatenate([white, jnp.zeros((1,) + white.shape[1:], white.dtype)], axis=0)
    lags = lag_table(BINS, MAXLAG, SAMPLES)
    width = CHANNELS // N_CHAN

    def one_family(pieces):
        index, mask = pieces
        spec = padded[index] * mask.astype(white.dtype)[None, :, None]
        energy = lax.optimization_barrier(jnp.sum(spec * spec, axis=(1, 2)))
        blocked = spec.reshape(SLOTS, N_CHAN, width, SAMPLES).transpose(1, 0, 2, 3)

        def add(total, piece):
            term = pair_terms(piece, paired_columns(piece), lags)
            return (total + term, None)
        total, _ = lax.scan(add, jnp.zeros((SLOTS, LAGS, SLOTS), white.dtype), blocked)
        norm = jnp.sqrt(energy + 1e-05)
        return total / (norm[:, None, None] * norm[None, None, :])
    return lax.map(one_family, (members.reshape(FAMS, SLOTS), channel_mask))
```

```python
import functools
import math

import jax
import jax.numpy as jnp
import numpy as np
from jax import lax
from jax.experimental import pallas as pl
from jax.experimental.pallas import tpu as pltpu
from jax.sharding import PartitionSpec as P

MAXLAG = 32
CAP = 16
LANES = 128
F16_SCALE = 16384.0
TINY = 1.2e-38
VMEM_LIMIT = 56 * 2**20
PITCH_PAD = 8
LONG = pl.CostEstimate(flops=10**14, bytes_accessed=1, transcendentals=0)
SHORT = pl.CostEstimate(flops=1, bytes_accessed=1, transcendentals=0)
FINISH_LIMIT = 40 * 2**20
F32 = jnp.float32
BF16 = jnp.bfloat16
IN_VMEM = pl.BlockSpec(memory_space=pltpu.VMEM)
IN_SMEM = pl.BlockSpec(memory_space=pltpu.SMEM)
IN_HBM = pl.BlockSpec(memory_space=pltpu.HBM)


def split(x):
    high = x.astype(BF16)
    return high, (x - high.astype(F32)).astype(BF16)


def split_table(table):
    high = table.astype(np.float32).astype(BF16)
    return high, (table - high.astype(np.float64)).astype(np.float32).astype(BF16)


def dot(a, b):
    return lax.dot_general(a, b, (((1,), (0,)), ((), ())), preferred_element_type=F32)


def dot_rows(a, b):
    return lax.dot_general(a, b, (((1,), (1,)), ((), ())), preferred_element_type=F32)


def transform_table(length):
    bins = length // 2
    angle = (np.arange(bins)[:, None] * np.arange(length)[None, :] % length) * (2.0 * math.pi / length)
    return np.concatenate(split_table(np.concatenate([np.cos(angle), -np.sin(angle)], axis=0)), axis=0)


def lag_rows():
    return (2 * MAXLAG + 1 + 7) // 8 * 8


def lag_table(length):
    bins = length // 2
    rows = lag_rows()
    shifts = np.arange(rows) - MAXLAG
    angle = (shifts[:, None] * np.arange(bins)[None, :] % length) * (2.0 * math.pi / length)
    table = np.concatenate([np.cos(angle), -np.sin(angle)], axis=1)
    high, low = split_table(table * (shifts <= MAXLAG)[:, None])
    return np.concatenate([high, low], axis=0)


def gather_kernel(owners, dests, me_ref, family_ref, wave_ref, *rest):
    outs = dict(zip(dests, rest[-5 - len(dests) : -5]))
    count, zero, buf, arrived, sent = rest[-5:]
    index = {d: n for n, d in enumerate(dests)}
    me = me_ref[0]
    zero[...] = jnp.zeros_like(zero)
    for f in range(owners):
        count[f] = 0

    def place(e, carry):
        f = family_ref[e]
        r = count[f]
        count[f] = r + 1
        d = jnp.bitwise_xor(f, me)
        spot = jnp.where(r < CAP // 2, 2 * r, 2 * r - CAP + 1)
        slot = d - dests[0]

        @pl.when((d >= dests[0]) & (d <= dests[-1]))
        def _():
            pltpu.make_async_copy(wave_ref.at[e], buf.at[slot, spot], arrived.at[slot]).start()

        return carry

    lax.fori_loop(0, family_ref.shape[0], place, 0, unroll=4)
    for d in dests:

        def fill(r, carry):
            spot = jnp.where(r < CAP // 2, 2 * r, 2 * r - CAP + 1)
            pltpu.make_async_copy(zero, buf.at[index[d], spot], arrived.at[index[d]]).start()
            return carry

        lax.fori_loop(count[jnp.bitwise_xor(me, d)], CAP, fill, 0)
    for d in dests:
        n = index[d]
        pltpu.make_async_copy(buf.at[n], buf.at[n], arrived.at[n]).wait()
        pltpu.make_async_copy(buf.at[n], outs[d], sent.at[n]).start()
    for d in dests:
        n = index[d]
        pltpu.make_async_copy(buf.at[n], outs[d], sent.at[n]).wait()


def gather(me, family_of, waveforms, owners, dests, after):
    shape = (CAP,) + waveforms.shape[1:]
    count = len(dests)
    return pl.pallas_call(
        functools.partial(gather_kernel, owners, dests),
        out_shape=[jax.ShapeDtypeStruct(shape, waveforms.dtype)] * count,
        in_specs=[IN_SMEM, IN_SMEM, IN_HBM] + [IN_HBM] * len(after),
        out_specs=[IN_HBM] * count,
        scratch_shapes=[
            pltpu.SMEM((owners,), jnp.int32),
            pltpu.VMEM(waveforms.shape[1:], waveforms.dtype),
            pltpu.VMEM((count,) + shape, waveforms.dtype),
            pltpu.SemaphoreType.DMA((count,)),
            pltpu.SemaphoreType.DMA((count,)),
        ],
        cost_estimate=SHORT,
        compiler_params=pltpu.CompilerParams(vmem_limit_bytes=VMEM_LIMIT),
        name="gather_slots",
    )(me, family_of, waveforms, *after)


def spot_of(event):
    return event % 2 * (CAP // 2) + event // 2


def code_of(tile):
    exponent = jnp.floor(jnp.log2(jnp.maximum(tile, TINY)))
    mantissa = tile * jnp.exp2(-exponent)
    high = mantissa.astype(BF16).astype(F32)
    return high, mantissa - high, exponent * (1.0 / 64.0)


def whiten_body(x_ref, table_ref, mask_ref, scratch, write):
    events, chans, length = x_ref.shape
    bins = length // 2
    cols = 2 * LANES
    step = cols // chans
    groups = events * chans // LANES
    row = lax.broadcasted_iota(jnp.int32, (bins, cols), 0)
    col = lax.broadcasted_iota(jnp.int32, (bins, cols), 1)
    near = (jnp.abs(row - jnp.bitwise_and(col, bins - 1)) <= 4).astype(F32).astype(BF16)
    count = jnp.minimum(row + 4, bins - 1) - jnp.maximum(row - 4, 0) + 1
    inverse = 1.0 / count.astype(F32)
    row = lax.broadcasted_iota(jnp.int32, (cols, cols), 0) // chans
    col = lax.broadcasted_iota(jnp.int32, (cols, cols), 1) // chans
    same = (row == col).astype(F32).astype(BF16)
    lane = jnp.bitwise_and(lax.broadcasted_iota(jnp.int32, (8, LANES), 1), CAP - 1)
    tile = jnp.zeros((8, LANES), F32)
    for n in range(events // step):
        x = x_ref[n * step : (n + 1) * step].reshape(cols, length)
        spec = dot_rows(table_ref[:length], x) + dot_rows(table_ref[length:], x)
        re = spec[:bins]
        im = spec[bins:]
        power = re * re + im * im
        high, low = split(power)
        smooth = dot(near, jnp.concatenate([high, low], axis=0))
        level = jnp.sum(power, axis=0, keepdims=True) * (0.1 / bins) + 1e-5
        scale = lax.rsqrt(smooth * inverse + level) * mask_ref[...]
        lane_energy = jnp.sum(power * (scale * scale), axis=0, keepdims=True)
        high, low = split(lane_energy)
        rest = (lane_energy - high.astype(F32) - low.astype(F32)).astype(BF16)
        parts = jnp.concatenate([high, low, rest] + [jnp.zeros_like(high)] * 13, axis=0)
        energy = jnp.sum(dot(parts, same), axis=0, keepdims=True)
        for e in range(step):
            value = jnp.broadcast_to(energy[:, e * chans : e * chans + 1], (8, LANES))
            tile = jnp.where(lane == spot_of(n * step + e), value, tile)
        unit = jnp.where(energy > TINY, lax.rsqrt(jnp.maximum(energy, TINY)), 0.0)
        factor = scale * unit
        re = re * factor
        im = im * factor
        for h in range(2):
            g = 2 * n + h
            scratch[g * bins : (g + 1) * bins] = re[:, h * LANES : (h + 1) * LANES]
            scratch[(groups + g) * bins : (groups + g + 1) * bins] = im[:, h * LANES : (h + 1) * LANES]
    first = lax.broadcasted_iota(jnp.int32, (groups, LANES), 1) < LANES // 2

    def relayout(k, carry):
        re = scratch[pl.ds(k, groups, stride=bins), :]
        im = scratch[pl.ds(groups * bins + k, groups, stride=bins), :]
        re_rolled = pltpu.roll(re, LANES // 2, 1)
        im_rolled = pltpu.roll(im, LANES // 2, 1)
        member = jnp.concatenate([jnp.where(first, re, im_rolled), jnp.where(first, re_rolled, im)], axis=0)
        write(k, *split(member))
        return carry

    lax.fori_loop(0, bins, relayout, 0, unroll=16)
    return tile


def whiten_kernel(count, table_hbm, mask_ref, *refs):
    x_hbm = refs[:count]
    m_hbm, e_ref = refs[-7 - 2 * count : -7 - count], refs[-7 - count : -7]
    x_ref, table_ref, m_ref, scratch, sem, x_sem, out_sem = refs[-7:]
    load = pltpu.make_async_copy(table_hbm, table_ref, sem)
    load.start()
    loads = [pltpu.make_async_copy(x_hbm[n], x_ref.at[n], x_sem.at[n]) for n in range(count)]
    for c in loads:
        c.start()
    load.wait()
    outs = []
    for n in range(count):
        loads[n].wait()

        def write(k, high, low):
            m_ref[n, k, :, :LANES] = high
            m_ref[n, k, :, LANES:] = low

        e_ref[n][...] = whiten_body(x_ref.at[n], table_ref, mask_ref, scratch.at[n % 2], write)
        outs.append(pltpu.make_async_copy(m_ref.at[n], m_hbm[n], out_sem.at[n]))
        outs[-1].start()
    for c in outs:
        c.wait()


def member_shapes(x):
    events, chans, length = x.shape
    bins = length // 2
    m = jax.ShapeDtypeStruct((bins, events, 2 * LANES), BF16)
    return m, (2 * events * chans // LANES * bins, LANES)


ENERGY = jax.ShapeDtypeStruct((8, LANES), F32)


def whiten(xs, table, mask, after):
    count = len(xs)
    m, scratch = member_shapes(xs[0])
    out = pl.pallas_call(
        functools.partial(whiten_kernel, count),
        out_shape=[m] * count + [ENERGY] * count,
        in_specs=[IN_HBM, IN_VMEM] + [IN_HBM] * (count + len(after)),
        out_specs=[IN_HBM] * count + [IN_VMEM] * count,
        scratch_shapes=[
            pltpu.VMEM((count,) + xs[0].shape, xs[0].dtype),
            pltpu.VMEM(table.shape, table.dtype),
            pltpu.VMEM((count,) + m.shape, m.dtype),
            pltpu.VMEM((2,) + scratch, F32),
            pltpu.SemaphoreType.DMA,
            pltpu.SemaphoreType.DMA((count,)),
            pltpu.SemaphoreType.DMA((count,)),
        ],
        cost_estimate=SHORT,
        compiler_params=pltpu.CompilerParams(vmem_limit_bytes=VMEM_LIMIT),
        name="whiten",
    )(table, mask, *xs, *after)
    return out[:count], out[count:]


def turn(m):
    half = LANES // 2
    return jnp.concatenate([m[:, half:LANES], -m[:, :half]], axis=1)


def pairs_body(me, new, members, table_ref, cross_ref, emit):
    bins, slots, _ = members.shape
    tiles = slots // LANES
    taus = table_ref.shape[0] // 2
    n = len(new) * CAP
    pitch = 2 * bins + PITCH_PAD

    def cross(k, carry):
        both = members[k]
        left = [members[k, pl.ds(place(me, d), CAP), :] for d in new]
        left = jnp.concatenate(left, axis=0)
        high = left[:, :LANES]
        low = left[:, LANES:]
        left = jnp.concatenate([high, turn(high), low, turn(low)], axis=0)
        right = jnp.concatenate([both[:, :LANES], both[:, LANES:]], axis=0)
        out = dot_rows(left, right)
        total = out[: 2 * n, :slots] + (out[: 2 * n, slots:] + out[2 * n :, :slots])
        for q in range(2):
            for t in range(tiles):
                part = total[q * n : (q + 1) * n, t * LANES : (t + 1) * LANES]
                cross_ref[t, pl.ds(q * bins + k, n, stride=pitch), :] = part
        return carry

    lax.fori_loop(0, bins, cross, 0, unroll=16 if n <= 32 else 8)
    table = table_ref[...]

    def lag(i, carry):
        for t in range(tiles):
            pair = cross_ref[t, pl.ds(pl.multiple_of(2 * i * pitch, 8), 2 * pitch), :]
            pair = jnp.concatenate([pair[: 2 * bins], pair[pitch : pitch + 2 * bins]], axis=1)
            high, low = split(pair)
            out = dot(table, high)
            out = out[:taus] + (out[taus:] + dot(table[:taus], low))
            for h in range(2):
                emit(2 * i + h, t, out[:, h * LANES : (h + 1) * LANES])
        return carry

    lax.fori_loop(0, n // 2, lag, 0, unroll=4)


def turn_lines(lines, codes, chan, turned, taus):
    tiles = lines.shape[0] // (CAP * taus)
    groups, parts = turned.shape[0], taus // 8
    rows = turned.shape[1] // parts
    for g in range(parts):
        for t in range(tiles):
            pieces = []
            for u in range(7, -1, -1):
                tau = 2 * MAXLAG - 8 * g - u
                if tau >= 0:
                    pieces.append(lines[pl.ds(t * CAP * taus + tau, CAP, stride=taus), :])
                else:
                    pieces.append(codes[min(-tau, len(codes)) - 1])
            value = jnp.concatenate(pieces, axis=0).T
            for c in range(LANES // rows):
                target = jnp.bitwise_xor(chan, t * (LANES // rows) + c)
                turned[target, g * rows : (g + 1) * rows] = value[c * rows : (c + 1) * rows]


def place(me, d):
    return pl.multiple_of(jnp.bitwise_xor(me, d) * CAP, CAP)


def load_members(me, ms, old, members, sem):
    copies = [
        pltpu.make_async_copy(ms[i], members.at[:, pl.ds(place(me, d), CAP), :], sem.at[i]) for i, d in enumerate(old)
    ]
    for c in copies:
        c.start()
    return copies


def slot_vector(me, tiles, slots):
    lane = lax.broadcasted_iota(jnp.int32, (8, slots), 1) // CAP
    value = jnp.zeros((8, slots), F32)
    for d, tile in tiles.items():
        value = jnp.where(lane == jnp.bitwise_xor(me, d), jnp.concatenate([tile] * (slots // LANES), axis=1), value)
    return value


def as_rows(value, ref):
    for t in range(value.shape[1] // LANES):
        part = jnp.broadcast_to(value[0:1, t * LANES : (t + 1) * LANES], (LANES, LANES))
        ref[t * LANES : (t + 1) * LANES] = part.T


def whiten_and_load(new, old, me, x_hbm, ms, tables, buffers, sems, keep):
    table_hbm, mask_ref = tables
    x_ref, table_ref, scratch, members = buffers
    load, x_sem, sem = sems
    table_load = pltpu.make_async_copy(table_hbm, table_ref, load)
    table_load.start()
    loads = [pltpu.make_async_copy(x_hbm[n], x_ref.at[n], x_sem.at[n]) for n in range(len(new))]
    for c in loads:
        c.start()
    copies = load_members(me, ms, old, members, sem)
    table_load.wait()
    tiles = {}
    for n, d in enumerate(new):
        where = place(me, d)
        loads[n].wait()

        def write(k, high, low):
            members[k, pl.ds(where, CAP), :LANES] = high
            members[k, pl.ds(where, CAP), LANES:] = low

        tiles[d] = whiten_body(x_ref.at[n], table_ref, mask_ref, scratch.at[n % 2], write)
        keep(n, members.at[:, pl.ds(where, CAP), :])
    for c in copies:
        c.wait()
    return tiles


def shared_scratch(x, new, old, table, slots, n):
    m, scratch = member_shapes(x)
    bins = m.shape[0]
    return [
        pltpu.VMEM((len(new),) + x.shape, x.dtype),
        pltpu.VMEM(table.shape, table.dtype),
        pltpu.VMEM((min(2, len(new)),) + scratch, F32),
        pltpu.VMEM((bins, slots, 2 * LANES), BF16),
        pltpu.VMEM((slots // LANES, n * (2 * bins + PITCH_PAD), LANES), F32),
        pltpu.SemaphoreType.DMA,
        pltpu.SemaphoreType.DMA((len(new),)),
        pltpu.SemaphoreType.DMA((len(old),)),
        pltpu.SemaphoreType.DMA((24,)),
    ]


def square_kernel(old, new, lines_of, more, me_ref, table_hbm, mask_ref, lag_ref, *refs):
    count = len(new)
    x_hbm, refs = refs[:count], refs[count:]
    ms, refs = refs[: len(old)], refs[len(old) :]
    given, refs = refs[: len(old)], refs[len(old) :]
    x_ref, table_ref, scratch, members, cross_ref, load, x_sem, sem, out_sem, rows_ref = refs[-10:]
    outs = refs[-10 - 1 - count * (1 + more) : -10]
    me, own = me_ref[0], me_ref[2]
    slots = members.shape[1]
    done = []

    def keep(n, block):
        if more:
            done.append(pltpu.make_async_copy(block, outs[1 + count + n], out_sem.at[8 + n]))
            done[-1].start()

    buffers = (x_ref, table_ref, scratch, members)
    tiles = whiten_and_load(new, old, me, x_hbm, ms, (table_hbm, mask_ref), buffers, (load, x_sem, sem), keep)
    for n, d in enumerate(new):
        outs[1 + n][...] = tiles[d]
    for d, ref in zip(old, given):
        tiles[d] = ref[...]
    codes = code_of(slot_vector(me, tiles, slots))

    def emit(row, t, part):
        rows_ref[row, :, t * LANES : (t + 1) * LANES] = part

    pairs_body(me, lines_of, members, lag_ref, cross_ref, emit)
    groups, rows = outs[0].shape[:2]
    first = lines_of[0] * CAP // rows
    for n in range(rows_ref.shape[0] // rows):
        for c, code in enumerate(codes):
            rows_ref[n * rows, 2 * MAXLAG + 1 + c : 2 * MAXLAG + 2 + c] = code[0:1]
        target = jnp.bitwise_xor(first + n, own)
        done.append(pltpu.make_async_copy(rows_ref.at[n * rows : (n + 1) * rows], outs[0].at[target], out_sem.at[n]))
        done[-1].start()
    if first + rows_ref.shape[0] // rows == groups - 1:
        target = jnp.bitwise_xor(groups - 1, own)
        done.append(pltpu.make_async_copy(rows_ref.at[:rows], outs[0].at[target], out_sem.at[groups - 1]))
        done[-1].start()
    for c in done:
        c.wait()


def square(me, xs, table, mask, lags, ms, energy, lines_of, slots, groups, more, after, filled):
    old, new = sorted(ms), sorted(xs)
    taus = lags.shape[0] // 2
    x = xs[new[0]]
    m, _ = member_shapes(x)
    n = len(lines_of) * CAP
    rows = jax.ShapeDtypeStruct((groups, slots // groups, taus, slots), F32)
    return pl.pallas_call(
        functools.partial(square_kernel, old, new, lines_of, more),
        out_shape=[rows] + [ENERGY] * len(new) + [m] * (more * len(new)),
        in_specs=[IN_SMEM, IN_HBM, IN_VMEM, IN_VMEM]
        + [IN_HBM] * (len(new) + len(old))
        + [IN_VMEM] * len(old)
        + [IN_HBM] * (len(after) + len(filled)),
        out_specs=[IN_HBM] + [IN_VMEM] * len(new) + [IN_HBM] * (more * len(new)),
        scratch_shapes=shared_scratch(x, new, old, table, slots, n)
        + [pltpu.VMEM((n, taus, slots), F32)],
        cost_estimate=SHORT,
        compiler_params=pltpu.CompilerParams(vmem_limit_bytes=VMEM_LIMIT),
        input_output_aliases={4 + len(new) + 2 * len(old) + len(after): 0} if filled else {},
        name="square",
    )(me, table, mask, lags, *[xs[d] for d in new], *[ms[d] for d in old], *[energy[d] for d in old], *after, *filled)


def step_kernel(old, new, final, me_ref, table_hbm, mask_ref, lag_ref, x_hbm, *refs):
    ms, refs = refs[: len(old)], refs[len(old) :]
    lines, turned_ref = refs[-2:]
    x_ref, table_ref, scratch, members, cross_ref, load, x_sem, sem, out_sem = refs[-11:-2]
    outs = refs[-11 - (2 if final else 4) : -11]
    me, chan = me_ref[0], me_ref[1]
    slots = members.shape[1]
    taus = lag_ref.shape[0] // 2
    done = []

    def start(source, target):
        done.append(pltpu.make_async_copy(source, target, out_sem.at[len(done)]))
        done[-1].start()

    def keep(n, block):
        if not final:
            start(block, outs[2])

    full_lines, full_turned = lines, turned_ref
    if final:
        kept_lines, kept_turned = refs[:2]
        cut, turned_cut = kept_lines.shape[0], kept_turned.shape[1]
        start(kept_lines, lines.at[:cut])
        start(kept_turned, turned_ref.at[:, :turned_cut])
        lines, turned_ref = lines.at[cut:], turned_ref.at[:, turned_cut:]
    buffers = (x_ref, table_ref, scratch, members)
    tiles = whiten_and_load([new], old, me, [x_hbm], ms, (table_hbm, mask_ref), buffers, (load, x_sem, sem), keep)
    tile = tiles[new]
    column = jnp.broadcast_to(tile[0:1], (LANES, LANES)).T[:CAP]

    def emit(row, t, part):
        lines[pl.ds(pl.multiple_of((t * CAP + row) * taus, 8), taus), :] = part

    pairs_body(me, [new], members, lag_ref, cross_ref, emit)
    if final:
        for c in done:
            c.wait()
    else:
        outs[3][...] = tile
    start(full_lines, outs[0])
    turn_lines(lines, code_of(column), chan, turned_ref, taus)
    start(full_turned, outs[1])
    for c in done[2:] if final else done:
        c.wait()


def step(me, x, table, mask, lags, ms, new, slots, groups, kept, after):
    old = sorted(ms)
    taus = lags.shape[0] // 2
    m, _ = member_shapes(x)
    final = len(kept) > 0
    count = 1 + (kept[0].shape[0] // (slots // LANES * CAP * taus) if final else 0)
    lines = jax.ShapeDtypeStruct((count * (slots // LANES) * CAP * taus, LANES), F32)
    turned = jax.ShapeDtypeStruct((groups, count * (taus // 8) * (slots // groups), LANES), F32)
    return pl.pallas_call(
        functools.partial(step_kernel, old, new, final),
        out_shape=[lines, turned] + ([] if final else [m, ENERGY]),
        in_specs=[IN_SMEM, IN_HBM, IN_VMEM, IN_VMEM] + [IN_HBM] * (1 + len(old) + len(kept) + len(after)),
        out_specs=[IN_HBM] * 2 + ([] if final else [IN_HBM, IN_VMEM]),
        scratch_shapes=shared_scratch(x, [new], old, table, slots, CAP)
        + [pltpu.VMEM(lines.shape, F32), pltpu.VMEM(turned.shape, F32)],
        cost_estimate=LONG if final else SHORT,
        compiler_params=pltpu.CompilerParams(vmem_limit_bytes=VMEM_LIMIT),
        name="step",
    )(me, table, mask, lags, x, *[ms[d] for d in old], *kept, *after)


def hold_kernel(*refs):
    del refs


def hold(xs, after):
    n = len(xs)
    return pl.pallas_call(
        hold_kernel,
        out_shape=[jax.ShapeDtypeStruct(x.shape, x.dtype) for x in xs],
        in_specs=[IN_HBM] * (n + len(after)),
        out_specs=[IN_HBM] * n,
        input_output_aliases={i: i for i in range(n)},
        cost_estimate=SHORT,
        name="hold",
    )(*xs, *after)


def finish_kernel(last, blocks, me_ref, *refs):
    out_hbm, out_ref, lines_sum, rows_ref, sem = refs[-5:]
    me, chan, own = me_ref[0], me_ref[1], me_ref[2]
    rows, lags, slots = out_ref.shape
    tiles = slots // LANES
    groups = slots // rows
    taus = lag_rows()
    parts = taus // 8
    base, late, turned = refs[:groups], refs[groups : 2 * groups], refs[2 * groups : 3 * groups]
    scale = [1.0] + [1.0 / F16_SCALE] * (groups - 1)
    lane = lax.broadcasted_iota(jnp.int32, (8, LANES), 1)

    def spread(line, v):
        part = jnp.where(lane < CAP, pltpu.roll(line, LANES - v * CAP, 1), 0.0)
        for shift in (CAP, 2 * CAP, 4 * CAP):
            part = part + pltpu.roll(part, shift, 1)
        return part

    def energy_of(high, low, exponent, e):
        return (high + low) * scale[e] * jnp.exp2(jnp.round(exponent * (64.0 * scale[e])))

    block_of = lax.broadcasted_iota(jnp.int32, (8, slots), 1) // CAP
    every, local = [], []
    for e in range(groups):
        local.append({})
        for n, d in enumerate(last):
            start = (n * parts + parts - 1) * rows
            line = turned[e][start : start + 8]
            local[e][d] = energy_of(spread(line, 6), spread(line, 5), spread(line, 4), e)
        codes = base[e][0, taus - 8 : taus]
        vector = jnp.broadcast_to(energy_of(codes[1:2], codes[2:3], codes[3:4], e), (8, slots))
        for d in last:
            wide = jnp.concatenate([local[e][d]] * tiles, axis=1)
            vector = jnp.where(block_of == jnp.bitwise_xor(me, d), wide, vector)
        every.append(vector)
    norm = lax.rsqrt(sum(every) + 1e-05)
    every = [jnp.sqrt(x) * norm for x in every]
    norms = {d: lax.rsqrt(sum(x[d] for x in local) + 1e-05) for d in last}
    local = [{d: jnp.sqrt(x[d]) * norms[d] for d in last} for x in local]
    for e in range(groups):
        as_rows(every[e] * scale[e], rows_ref.at[e])
    mine = [rows_ref[e, pl.ds(pl.multiple_of(chan * rows, 8), rows), :] for e in range(groups)]
    for n, d in enumerate(last):
        weight = [mine[e] * local[e][d][0:1] for e in range(groups)]
        shift = (jnp.bitwise_xor(me, d) * CAP + LANES - 7 * CAP) % LANES
        for g in range(parts):
            total = 0.0
            for e in range(groups):
                start = (n * parts + g) * rows
                total = total + turned[e][start : start + rows] * weight[e]
            lines_sum[n, g] = pltpu.roll(total, shift, 1)

    def emit(h, from_base):
        d_row = own * blocks + h
        b_row = jnp.bitwise_and(jnp.bitwise_xor(me, d_row), blocks - 1)
        d_late = last[h]

        def one_row(r, carry):
            target = b_row * CAP + r
            slot = jnp.bitwise_xor(me, d_row) * CAP + r
            weight = []
            for e in range(groups):
                row = rows_ref[e, pl.ds(slot, 1), :]
                weight.append(jnp.concatenate([row] * tiles, axis=1) * every[e][0:1])
            for g in range(parts):
                value = 0.0
                for e in range(groups):
                    if from_base:
                        part = base[e][h * CAP + r, 8 * g : 8 * g + 8]
                    else:
                        pieces = []
                        for t in range(tiles):
                            start = pl.multiple_of(((h * tiles + t) * CAP + r) * taus + 8 * g, 8)
                            pieces.append(late[e][pl.ds(start, 8), :])
                        part = jnp.concatenate(pieces, axis=1)
                    value = value + part * weight[e]
                for n, d in enumerate(last):
                    if not from_base and d <= d_late:
                        continue
                    line = jnp.broadcast_to(lines_sum[n, g, pl.ds(target, 1), :], (8, LANES))
                    line = pltpu.roll(line, 0, 1, stride=CAP, stride_axis=0)
                    line = jnp.concatenate([line] * tiles, axis=1)
                    value = jnp.where(block_of == jnp.bitwise_xor(me, d), line, value)
                stop = min(8, lags - 8 * g)
                out_ref[target, 8 * g : 8 * g + stop] = value[:stop]
            return carry

        lax.fori_loop(0, CAP, one_row, 0, unroll=2)

    copies = []
    for h in range(blocks):

        @pl.when(own < groups - 1)
        def _():
            emit(h, True)

        @pl.when(own == groups - 1)
        def _():
            emit(h, False)

        b_row = jnp.bitwise_and(jnp.bitwise_xor(me, own * blocks + h), blocks - 1)
        part = pl.ds(b_row * CAP, CAP)
        copies.append(pltpu.make_async_copy(out_ref.at[part], out_hbm.at[part], sem.at[h]))
        copies[-1].start()
    for c in copies:
        c.wait()


def finish(me, base, late, turned, last, blocks):
    rows, taus, slots = base[0].shape
    groups = slots // rows
    shape = (rows, 2 * MAXLAG + 1, slots)
    return pl.pallas_call(
        functools.partial(finish_kernel, last, blocks),
        out_shape=jax.ShapeDtypeStruct(shape, F32),
        in_specs=[IN_SMEM] + [IN_VMEM] * (3 * groups),
        out_specs=IN_HBM,
        scratch_shapes=[
            pltpu.VMEM(shape, F32),
            pltpu.VMEM((len(last), taus // 8, rows, LANES), F32),
            pltpu.VMEM((groups, slots, LANES), F32),
            pltpu.SemaphoreType.DMA((blocks,)),
        ],
        cost_estimate=SHORT,
        compiler_params=pltpu.CompilerParams(vmem_limit_bytes=FINISH_LIMIT),
        name="finish",
    )(me, *base, *late, *turned)


def local(waveforms, family_of, channel_mask):
    owners = lax.axis_size("fam")
    groups = lax.axis_size("chan")
    blocks = owners // groups
    slots = owners * CAP
    rows = blocks * CAP
    chans, length = waveforms.shape[1:]
    fam = lax.axis_index("fam")
    chan = lax.axis_index("chan")
    own = jnp.bitwise_xor(chan, fam // blocks)
    me = jnp.stack([fam, chan, own, fam // blocks]).astype(jnp.int32)

    half_lanes = LANES // 2
    mask = jnp.pad(channel_mask.astype(F32), ((0, 0), (0, half_lanes - chans)))
    mask = jnp.tile(mask, (1, 4))
    table = jnp.asarray(transform_table(length))
    lags = jnp.asarray(lag_table(length))
    taus = lag_rows()

    half = owners // 2
    last = list(range(owners - blocks, owners))
    early = [d for d in range(owners) if d not in last]
    first = list(range(half, half + blocks))
    sends, inbox, ms, energy = {}, {}, {}, {}
    widen = ((0, 0), (0, half_lanes - chans), (0, 0))

    def collect(dests, after):
        sends.update(zip(dests, gather(me, family_of, waveforms, owners, dests, after)))

    def post(d):
        inbox[d] = jnp.pad(lax.ppermute(sends[d], "fam", [(i, i ^ d) for i in range(owners)]), widen)

    def chan_permute(x, e):
        return lax.ppermute(x, "chan", [(i, i ^ e) for i in range(groups)])

    partners = list(range(groups - 1, 0, -1))

    collect(first, [])
    for d in first:
        post(d)
    collect(list(range(half)), [sends[first[0]]])
    for d in range(1, half):
        post(d)
    inbox[0] = jnp.pad(sends[0], widen)
    remaining = list(range(half + blocks, owners))
    collect(remaining, [inbox[d] for d in range(1, half)])
    for d in remaining:
        post(d)
    after = [sends[first[0]]]
    middle = [d for d in early if d >= half]
    rest = [d for d in early if d < half]
    for start in [0, 1] + list(range(4, half, 4)):
        if start == 1:
            after = after + [sends[remaining[0]]]
        part = list(range(start, min({0: 1, 1: 4}.get(start, start + 4), half)))
        got_m, got_e = whiten([inbox[d] for d in part], table, mask, after)
        ms.update(zip(part, got_m))
        energy.update(zip(part, got_e))
        after = [got_e[0]]

    limit = max(1, 16 * 2**20 // (CAP * length * slots * 4))
    per_call = max(n for n in range(blocks, len(early) + 1, blocks) if len(early) % n == 0 and n <= max(limit, blocks))
    held = {d: ms[d] for d in rest}
    filled = []
    for start in range(0, len(early), per_call):
        lines_of = early[start : start + per_call]
        xs = {d: inbox[d] for d in middle}
        more = int(start == 0)
        result = square(me, xs, table, mask, lags, held, energy, lines_of, slots, groups, more, after, filled)
        filled = [result[0]]
        if more:
            known = dict(zip(middle, result[1:]))
            ms.update(zip(middle, result[1 + len(middle) :]))
            after = [result[1]]
    energy.update(known)

    def narrow(x):
        return (x * F16_SCALE).astype(jnp.float16)

    early_rows = filled[0].reshape(groups, rows * taus, slots)
    sent = {e: chan_permute(narrow(early_rows[e]), e) for e in partners}

    kept = []
    for n, d in enumerate(last):
        result = step(me, inbox[d], table, mask, lags, ms, d, slots, groups, kept, after)
        kept = result[:2]
        after = []
        if n < len(last) - 1:
            ms[d], energy[d] = result[2:]
    late, turned = hold(kept, [sum(sent[e][:8].astype(F32) for e in partners)])

    def widen_f32(x, shape):
        return x.astype(F32).reshape(shape)

    base_parts, late_parts, turned_parts = [filled[0][0]], [late], [turned[0]]
    small = narrow(late)
    got_late, got_turned = {}, {}
    for e in partners:
        to_owner = []
        for f in range(owners):
            owner = (f // blocks) ^ (groups - 1)
            to_owner.append(((owner ^ e) * owners + f, owner * owners + f))
        got_late[e] = lax.ppermute(small, ("chan", "fam"), to_owner).astype(F32)
        got_turned[e] = chan_permute(narrow(turned[e]), e).astype(F32)
    for e in range(1, groups):
        base_parts.append(widen_f32(sent[e], (rows, taus, slots)))
        late_parts.append(got_late[e])
        turned_parts.append(got_turned[e])
    return finish(me, base_parts, late_parts, turned_parts, last, blocks)[None]


def solution(mesh):
    in_specs = (P("fam", "chan", None), P("fam"), P("fam", "chan"))
    out_specs = P("fam", "chan", None, None)
    return jax.shard_map(local, mesh=mesh, in_specs=in_specs, out_specs=out_specs, check_vma=False)
```

```python
import functools
import math

import jax
import jax.numpy as jnp
import numpy as np
from jax import lax
from jax.experimental import pallas as pl
from jax.experimental.pallas import tpu as pltpu
from jax.sharding import PartitionSpec as P

MAXLAG = 32
CAP = 16
LANES = 128
F16_SCALE = 16384.0
TINY = 1.2e-38
VMEM_LIMIT = 56 * 2**20
PITCH_PAD = 8
LOAD_PARTS = 4
LONG = pl.CostEstimate(flops=10**14, bytes_accessed=1, transcendentals=0)
SHORT = pl.CostEstimate(flops=1, bytes_accessed=1, transcendentals=0)
FINISH_LIMIT = 40 * 2**20
F32 = jnp.float32
BF16 = jnp.bfloat16
IN_VMEM = pl.BlockSpec(memory_space=pltpu.VMEM)
IN_SMEM = pl.BlockSpec(memory_space=pltpu.SMEM)
IN_HBM = pl.BlockSpec(memory_space=pltpu.HBM)


def split(x):
    high = x.astype(BF16)
    return high, (x - high.astype(F32)).astype(BF16)


def split_table(table):
    high = table.astype(np.float32).astype(BF16)
    return high, (table - high.astype(np.float64)).astype(np.float32).astype(BF16)


def dot(a, b):
    return lax.dot_general(a, b, (((1,), (0,)), ((), ())), preferred_element_type=F32)


def dot_rows(a, b):
    return lax.dot_general(a, b, (((1,), (1,)), ((), ())), preferred_element_type=F32)


def transform_table(length):
    bins = length // 2
    angle = (np.arange(bins)[:, None] * np.arange(length)[None, :] % length) * (2.0 * math.pi / length)
    return np.concatenate(split_table(np.concatenate([np.cos(angle), -np.sin(angle)], axis=0)), axis=0)


def lag_rows():
    return (2 * MAXLAG + 1 + 7) // 8 * 8


def lag_table(length):
    bins = length // 2
    rows = lag_rows()
    shifts = np.arange(rows) - MAXLAG
    angle = (shifts[:, None] * np.arange(bins)[None, :] % length) * (2.0 * math.pi / length)
    table = np.concatenate([np.cos(angle), -np.sin(angle)], axis=1)
    high, low = split_table(table * (shifts <= MAXLAG)[:, None])
    return np.concatenate([high, low], axis=0)


def gather_kernel(owners, dests, me_ref, family_ref, wave_ref, *rest):
    outs = dict(zip(dests, rest[-5 - len(dests) : -5]))
    count, zero, buf, arrived, sent = rest[-5:]
    index = {d: n for n, d in enumerate(dests)}
    me = me_ref[0]
    zero[...] = jnp.zeros_like(zero)
    for f in range(owners):
        count[f] = 0

    def place(e, carry):
        f = family_ref[e]
        r = count[f]
        count[f] = r + 1
        d = jnp.bitwise_xor(f, me)
        spot = jnp.where(r < CAP // 2, 2 * r, 2 * r - CAP + 1)
        slot = d - dests[0]

        @pl.when((d >= dests[0]) & (d <= dests[-1]))
        def _():
            pltpu.make_async_copy(wave_ref.at[e], buf.at[slot, spot], arrived.at[slot]).start()

        return carry

    lax.fori_loop(0, family_ref.shape[0], place, 0, unroll=4)
    for d in dests:

        def fill(r, carry):
            spot = jnp.where(r < CAP // 2, 2 * r, 2 * r - CAP + 1)
            pltpu.make_async_copy(zero, buf.at[index[d], spot], arrived.at[index[d]]).start()
            return carry

        lax.fori_loop(count[jnp.bitwise_xor(me, d)], CAP, fill, 0)
    for d in dests:
        n = index[d]
        pltpu.make_async_copy(buf.at[n], buf.at[n], arrived.at[n]).wait()
        pltpu.make_async_copy(buf.at[n], outs[d], sent.at[n]).start()
    for d in dests:
        n = index[d]
        pltpu.make_async_copy(buf.at[n], outs[d], sent.at[n]).wait()


def gather(me, family_of, waveforms, owners, dests, after):
    shape = (CAP,) + waveforms.shape[1:]
    count = len(dests)
    return pl.pallas_call(
        functools.partial(gather_kernel, owners, dests),
        out_shape=[jax.ShapeDtypeStruct(shape, waveforms.dtype)] * count,
        in_specs=[IN_SMEM, IN_SMEM, IN_HBM] + [IN_HBM] * len(after),
        out_specs=[IN_HBM] * count,
        scratch_shapes=[
            pltpu.SMEM((owners,), jnp.int32),
            pltpu.VMEM(waveforms.shape[1:], waveforms.dtype),
            pltpu.VMEM((count,) + shape, waveforms.dtype),
            pltpu.SemaphoreType.DMA((count,)),
            pltpu.SemaphoreType.DMA((count,)),
        ],
        cost_estimate=SHORT,
        compiler_params=pltpu.CompilerParams(vmem_limit_bytes=VMEM_LIMIT),
        name="gather_slots",
    )(me, family_of, waveforms, *after)


def spot_of(event):
    return event % 2 * (CAP // 2) + event // 2


def code_of(tile):
    exponent = jnp.floor(jnp.log2(jnp.maximum(tile, TINY)))
    mantissa = tile * jnp.exp2(-exponent)
    high = mantissa.astype(BF16).astype(F32)
    return high, mantissa - high, exponent * (1.0 / 64.0)


def whiten_body(x_ref, table_ref, mask_ref, scratch, write):
    events, chans, length = x_ref.shape
    bins = length // 2
    cols = 2 * LANES
    step = cols // chans
    groups = events * chans // LANES
    row = lax.broadcasted_iota(jnp.int32, (bins, cols), 0)
    col = lax.broadcasted_iota(jnp.int32, (bins, cols), 1)
    near = (jnp.abs(row - jnp.bitwise_and(col, bins - 1)) <= 4).astype(F32).astype(BF16)
    count = jnp.minimum(row + 4, bins - 1) - jnp.maximum(row - 4, 0) + 1
    inverse = 1.0 / count.astype(F32)
    row = lax.broadcasted_iota(jnp.int32, (cols, cols), 0) // chans
    col = lax.broadcasted_iota(jnp.int32, (cols, cols), 1) // chans
    same = (row == col).astype(F32).astype(BF16)
    lane = jnp.bitwise_and(lax.broadcasted_iota(jnp.int32, (8, LANES), 1), CAP - 1)
    tile = jnp.zeros((8, LANES), F32)
    for n in range(events // step):
        x = x_ref[n * step : (n + 1) * step].reshape(cols, length)
        spec = dot_rows(table_ref[:length], x) + dot_rows(table_ref[length:], x)
        re = spec[:bins]
        im = spec[bins:]
        power = re * re + im * im
        high, low = split(power)
        smooth = dot(near, jnp.concatenate([high, low], axis=0))
        level = jnp.sum(power, axis=0, keepdims=True) * (0.1 / bins) + 1e-5
        scale = lax.rsqrt(smooth * inverse + level) * mask_ref[...]
        lane_energy = jnp.sum(power * (scale * scale), axis=0, keepdims=True)
        high, low = split(lane_energy)
        rest = (lane_energy - high.astype(F32) - low.astype(F32)).astype(BF16)
        parts = jnp.concatenate([high, low, rest] + [jnp.zeros_like(high)] * 13, axis=0)
        energy = jnp.sum(dot(parts, same), axis=0, keepdims=True)
        for e in range(step):
            value = jnp.broadcast_to(energy[:, e * chans : e * chans + 1], (8, LANES))
            tile = jnp.where(lane == spot_of(n * step + e), value, tile)
        unit = jnp.where(energy > TINY, lax.rsqrt(jnp.maximum(energy, TINY)), 0.0)
        factor = scale * unit
        re = re * factor
        im = im * factor
        for h in range(2):
            g = 2 * n + h
            scratch[g * bins : (g + 1) * bins] = re[:, h * LANES : (h + 1) * LANES]
            scratch[(groups + g) * bins : (groups + g + 1) * bins] = im[:, h * LANES : (h + 1) * LANES]
    first = lax.broadcasted_iota(jnp.int32, (groups, LANES), 1) < LANES // 2

    def relayout(k, carry):
        re = scratch[pl.ds(k, groups, stride=bins), :]
        im = scratch[pl.ds(groups * bins + k, groups, stride=bins), :]
        re_rolled = pltpu.roll(re, LANES // 2, 1)
        im_rolled = pltpu.roll(im, LANES // 2, 1)
        member = jnp.concatenate([jnp.where(first, re, im_rolled), jnp.where(first, re_rolled, im)], axis=0)
        write(k, *split(member))
        return carry

    lax.fori_loop(0, bins, relayout, 0, unroll=32)
    return tile


def whiten_kernel(ds, table_hbm, mask_ref, *refs):
    count = len(ds)
    x_hbm = refs[:count]
    m_hbm, e_ref = refs[-8 - count], refs[-7 - count : -7]
    x_ref, table_ref, m_ref, scratch, sem, x_sem, out_sem = refs[-7:]
    load = pltpu.make_async_copy(table_hbm, table_ref, sem)
    load.start()
    loads = [pltpu.make_async_copy(x_hbm[n], x_ref.at[n], x_sem.at[n]) for n in range(count)]
    for c in loads:
        c.start()
    load.wait()
    outs = []
    for n, d in enumerate(ds):
        loads[n].wait()

        def write(k, high, low):
            m_ref[n, k, :, :LANES] = high
            m_ref[n, k, :, LANES:] = low

        e_ref[n][...] = whiten_body(x_ref.at[n], table_ref, mask_ref, scratch.at[n % 2], write)
        outs.append(pltpu.make_async_copy(m_ref.at[n], m_hbm.at[d], out_sem.at[n]))
        outs[-1].start()
    for c in outs:
        c.wait()


def member_shapes(x):
    events, chans, length = x.shape
    bins = length // 2
    m = jax.ShapeDtypeStruct((bins, events, 2 * LANES), BF16)
    return m, (2 * events * chans // LANES * bins, LANES)


ENERGY = jax.ShapeDtypeStruct((8, LANES), F32)


def whiten(xs, table, mask, owners, filled, after):
    ds = sorted(xs)
    count = len(ds)
    m, scratch = member_shapes(xs[ds[0]])
    out = pl.pallas_call(
        functools.partial(whiten_kernel, ds),
        out_shape=[jax.ShapeDtypeStruct((owners,) + m.shape, m.dtype)] + [ENERGY] * count,
        in_specs=[IN_HBM, IN_VMEM] + [IN_HBM] * (count + len(after) + len(filled)),
        out_specs=[IN_HBM] + [IN_VMEM] * count,
        scratch_shapes=[
            pltpu.VMEM((count,) + xs[ds[0]].shape, xs[ds[0]].dtype),
            pltpu.VMEM(table.shape, table.dtype),
            pltpu.VMEM((count,) + m.shape, m.dtype),
            pltpu.VMEM((2,) + scratch, F32),
            pltpu.SemaphoreType.DMA,
            pltpu.SemaphoreType.DMA((count,)),
            pltpu.SemaphoreType.DMA((count,)),
        ],
        cost_estimate=SHORT,
        input_output_aliases={2 + count + len(after): 0} if filled else {},
        compiler_params=pltpu.CompilerParams(vmem_limit_bytes=VMEM_LIMIT),
        name="whiten",
    )(table, mask, *[xs[d] for d in ds], *after, *filled)
    return out[0], dict(zip(ds, out[1:]))


def turn(m):
    half = LANES // 2
    return jnp.concatenate([m[:, half:LANES], -m[:, :half]], axis=1)


def pairs_body(me, new, members, table_ref, cross_ref, copies, emit, ready):
    count, bins, _, _ = members.shape
    slots = count * CAP
    tiles = slots // LANES
    taus = table_ref.shape[0] // 2
    n = len(new) * CAP
    pitch = 2 * bins + PITCH_PAD

    def cross(k, carry):
        both = jnp.concatenate([members[jnp.bitwise_xor(me, b), k] for b in range(count)], axis=0)
        left = jnp.concatenate([members[d, k] for d in new], axis=0)
        high = left[:, :LANES]
        low = left[:, LANES:]
        left = jnp.concatenate([high, turn(high), low, turn(low)], axis=0)
        right = jnp.concatenate([both[:, :LANES], both[:, LANES:]], axis=0)
        out = dot_rows(left, right)
        total = out[: 2 * n, :slots] + (out[: 2 * n, slots:] + out[2 * n :, :slots])
        for q in range(2):
            for t in range(tiles):
                part = total[q * n : (q + 1) * n, t * LANES : (t + 1) * LANES]
                cross_ref[t, pl.ds(q * bins + k, n, stride=pitch), :] = part
        return carry

    step = bins // LOAD_PARTS
    for p in range(LOAD_PARTS):
        copies[p].wait()
        lax.fori_loop(p * step, (p + 1) * step, cross, 0, unroll=16)
    table = table_ref[...]

    def lag(i, carry):
        for t in range(tiles):
            pair = cross_ref[t, pl.ds(pl.multiple_of(2 * i * pitch, 8), 2 * pitch), :]
            pair = jnp.concatenate([pair[: 2 * bins], pair[pitch : pitch + 2 * bins]], axis=1)
            high, low = split(pair)
            out = dot(table, high)
            out = out[:taus] + (out[taus:] + dot(table[:taus], low))
            for h in range(2):
                emit(2 * i + h, t, out[:, h * LANES : (h + 1) * LANES])
        return carry

    for start in range(0, n // 2, CAP):
        stop = min(start + CAP, n // 2)
        lax.fori_loop(start, stop, lag, 0, unroll=8)
        ready(2 * stop)


def turn_lines(lines, codes, chan, turned, taus):
    tiles = lines.shape[0] // (CAP * taus)
    groups, parts = turned.shape[0], taus // 8
    rows = turned.shape[1] // parts
    for g in range(parts):
        for t in range(tiles):
            pieces = []
            for u in range(7, -1, -1):
                tau = 2 * MAXLAG - 8 * g - u
                if tau >= 0:
                    pieces.append(lines[pl.ds(t * CAP * taus + tau, CAP, stride=taus), :])
                else:
                    pieces.append(codes[min(-tau, len(codes)) - 1])
            value = jnp.concatenate(pieces, axis=0).T
            for c in range(LANES // rows):
                target = jnp.bitwise_xor(chan, t * (LANES // rows) + c)
                turned[target, g * rows : (g + 1) * rows] = value[c * rows : (c + 1) * rows]


def place(me, d):
    return pl.multiple_of(jnp.bitwise_xor(me, d) * CAP, CAP)


def load_members(m_hbm, count, members, sem):
    step = members.shape[1] // LOAD_PARTS
    copies = []
    for p in range(LOAD_PARTS):
        part = pl.ds(p * step, step)
        source, target = m_hbm.at[pl.ds(0, count), part], members.at[pl.ds(0, count), part]
        copies.append(pltpu.make_async_copy(source, target, sem.at[p]))
        copies[-1].start()
    return copies


def slot_vector(me, tiles, slots):
    lane = lax.broadcasted_iota(jnp.int32, (8, slots), 1) // CAP
    value = jnp.zeros((8, slots), F32)
    for d, tile in tiles.items():
        value = jnp.where(lane == jnp.bitwise_xor(me, d), jnp.concatenate([tile] * (slots // LANES), axis=1), value)
    return value


def as_rows(value, ref):
    for t in range(value.shape[1] // LANES):
        part = jnp.broadcast_to(value[0:1, t * LANES : (t + 1) * LANES], (LANES, LANES))
        ref[t * LANES : (t + 1) * LANES] = part.T


def whiten_and_load(new, count, me, x_hbm, m_hbm, tables, buffers, sems, keep):
    table_hbm, mask_ref = tables
    x_ref, table_ref, scratch, members = buffers
    load, x_sem, sem = sems
    table_load = pltpu.make_async_copy(table_hbm, table_ref, load)
    table_load.start()
    loads = [pltpu.make_async_copy(x_hbm[n], x_ref.at[n], x_sem.at[n]) for n in range(len(new))]
    for c in loads:
        c.start()
    copies = load_members(m_hbm, count, members, sem)
    table_load.wait()
    tiles = {}
    for n, d in enumerate(new):
        loads[n].wait()

        def write(k, high, low):
            members[d, k, :, :LANES] = high
            members[d, k, :, LANES:] = low

        tiles[d] = whiten_body(x_ref.at[n], table_ref, mask_ref, scratch.at[n % 2], write)
        keep(d, members.at[d])
    return tiles, copies


def shared_scratch(x, new, table, slots, n):
    m, scratch = member_shapes(x)
    bins = m.shape[0]
    return [
        pltpu.VMEM((len(new),) + x.shape, x.dtype),
        pltpu.VMEM(table.shape, table.dtype),
        pltpu.VMEM((min(2, len(new)),) + scratch, F32),
        pltpu.VMEM((slots // CAP, bins, CAP, 2 * LANES), BF16),
        pltpu.VMEM((slots // LANES, n * (2 * bins + PITCH_PAD), LANES), F32),
        pltpu.SemaphoreType.DMA,
        pltpu.SemaphoreType.DMA((len(new),)),
        pltpu.SemaphoreType.DMA((LOAD_PARTS,)),
        pltpu.SemaphoreType.DMA((24,)),
    ]


def square_kernel(old, new, lines_of, more, me_ref, table_hbm, mask_ref, lag_ref, *refs):
    count = len(new)
    x_hbm, refs = refs[:count], refs[count:]
    m_hbm, refs = refs[0], refs[1:]
    given, refs = refs[: len(old)], refs[len(old) :]
    x_ref, table_ref, scratch, members, cross_ref, load, x_sem, sem, out_sem, rows_ref = refs[-10:]
    outs = refs[-10 - 1 - count - more : -10]
    me, own = me_ref[0], me_ref[2]
    slots = members.shape[0] * CAP
    done = []

    def keep(d, block):
        if more:
            done.append(pltpu.make_async_copy(block, outs[1 + count].at[d], out_sem.at[8 + len(done)]))
            done[-1].start()

    buffers = (x_ref, table_ref, scratch, members)
    sems = (load, x_sem, sem)
    tables = (table_hbm, mask_ref)
    tiles, copies = whiten_and_load(new, len(old), me, x_hbm, m_hbm, tables, buffers, sems, keep)
    for n, d in enumerate(new):
        outs[1 + n][...] = tiles[d]
    for d, ref in zip(old, given):
        tiles[d] = ref[...]
    codes = code_of(slot_vector(me, tiles, slots))

    def emit(row, t, part):
        rows_ref[row, :, t * LANES : (t + 1) * LANES] = part

    groups, rows = outs[0].shape[:2]
    first = lines_of[0] * CAP // rows

    def ready(stop):
        if stop % rows == 0:
            n = stop // rows - 1
            for c, code in enumerate(codes):
                rows_ref[n * rows, 2 * MAXLAG + 1 + c : 2 * MAXLAG + 2 + c] = code[0:1]
            target = jnp.bitwise_xor(first + n, own)
            part = rows_ref.at[n * rows : (n + 1) * rows]
            done.append(pltpu.make_async_copy(part, outs[0].at[target], out_sem.at[n]))
            done[-1].start()

    pairs_body(me, lines_of, members, lag_ref, cross_ref, copies, emit, ready)
    if first + rows_ref.shape[0] // rows == groups - 1:
        target = jnp.bitwise_xor(groups - 1, own)
        done.append(pltpu.make_async_copy(rows_ref.at[:rows], outs[0].at[target], out_sem.at[groups - 1]))
        done[-1].start()
    for c in done:
        c.wait()


def square(me, xs, table, mask, lags, ms, energy, lines_of, slots, groups, more, after, filled):
    old, new = sorted(energy), sorted(xs)
    taus = lags.shape[0] // 2
    x = xs[new[0]]
    n = len(lines_of) * CAP
    rows = jax.ShapeDtypeStruct((groups, slots // groups, taus, slots), F32)
    members = jax.ShapeDtypeStruct(ms.shape, ms.dtype)
    aliases = {4 + len(new): 1 + len(new)} if more else {}
    if filled:
        aliases[5 + len(new) + len(old) + len(after)] = 0
    return pl.pallas_call(
        functools.partial(square_kernel, old, new, lines_of, more),
        out_shape=[rows] + [ENERGY] * len(new) + [members] * more,
        in_specs=[IN_SMEM, IN_HBM, IN_VMEM, IN_VMEM]
        + [IN_HBM] * (len(new) + 1)
        + [IN_VMEM] * len(old)
        + [IN_HBM] * (len(after) + len(filled)),
        out_specs=[IN_HBM] + [IN_VMEM] * len(new) + [IN_HBM] * more,
        scratch_shapes=shared_scratch(x, new, table, slots, n) + [pltpu.VMEM((n, taus, slots), F32)],
        cost_estimate=SHORT,
        input_output_aliases=aliases,
        compiler_params=pltpu.CompilerParams(vmem_limit_bytes=VMEM_LIMIT),
        name="square",
    )(me, table, mask, lags, *[xs[d] for d in new], ms, *[energy[d] for d in old], *after, *filled)


def step_kernel(new, final, me_ref, table_hbm, mask_ref, lag_ref, x_hbm, m_hbm, *refs):
    lines, turned_ref = refs[-2:]
    x_ref, table_ref, scratch, members, cross_ref, load, x_sem, sem, out_sem = refs[-11:-2]
    outs = refs[-11 - (2 if final else 4) : -11]
    me, chan = me_ref[0], me_ref[1]
    slots = members.shape[0] * CAP
    taus = lag_ref.shape[0] // 2
    done = []

    def start(source, target):
        done.append(pltpu.make_async_copy(source, target, out_sem.at[len(done)]))
        done[-1].start()

    def keep(d, block):
        if not final:
            start(block, outs[2].at[d])

    full_lines, full_turned = lines, turned_ref
    if final:
        kept_lines, kept_turned = refs[:2]
        cut, turned_cut = kept_lines.shape[0], kept_turned.shape[1]
        start(kept_lines, lines.at[:cut])
        start(kept_turned, turned_ref.at[:, :turned_cut])
        lines, turned_ref = lines.at[cut:], turned_ref.at[:, turned_cut:]
    buffers = (x_ref, table_ref, scratch, members)
    sems = (load, x_sem, sem)
    tiles, copies = whiten_and_load([new], new, me, [x_hbm], m_hbm, (table_hbm, mask_ref), buffers, sems, keep)
    tile = tiles[new]
    column = jnp.broadcast_to(tile[0:1], (LANES, LANES)).T[:CAP]

    def emit(row, t, part):
        lines[pl.ds(pl.multiple_of((t * CAP + row) * taus, 8), taus), :] = part

    pairs_body(me, [new], members, lag_ref, cross_ref, copies, emit, lambda stop: None)
    if final:
        for c in done:
            c.wait()
    else:
        outs[3][...] = tile
    start(full_lines, outs[0])
    turn_lines(lines, code_of(column), chan, turned_ref, taus)
    start(full_turned, outs[1])
    for c in done[2:] if final else done:
        c.wait()


def step(me, x, table, mask, lags, ms, new, slots, groups, kept, after):
    taus = lags.shape[0] // 2
    final = len(kept) > 0
    count = 1 + (kept[0].shape[0] // (slots // LANES * CAP * taus) if final else 0)
    lines = jax.ShapeDtypeStruct((count * (slots // LANES) * CAP * taus, LANES), F32)
    turned = jax.ShapeDtypeStruct((groups, count * (taus // 8) * (slots // groups), LANES), F32)
    members = jax.ShapeDtypeStruct(ms.shape, ms.dtype)
    return pl.pallas_call(
        functools.partial(step_kernel, new, final),
        out_shape=[lines, turned] + ([] if final else [members, ENERGY]),
        in_specs=[IN_SMEM, IN_HBM, IN_VMEM, IN_VMEM] + [IN_HBM] * (2 + len(kept) + len(after)),
        out_specs=[IN_HBM] * 2 + ([] if final else [IN_HBM, IN_VMEM]),
        scratch_shapes=shared_scratch(x, [new], table, slots, CAP)
        + [pltpu.VMEM(lines.shape, F32), pltpu.VMEM(turned.shape, F32)],
        cost_estimate=LONG if final else SHORT,
        input_output_aliases={} if final else {5: 2},
        compiler_params=pltpu.CompilerParams(vmem_limit_bytes=VMEM_LIMIT),
        name="step",
    )(me, table, mask, lags, x, ms, *kept, *after)


def hold_kernel(*refs):
    del refs


def hold(xs, after):
    n = len(xs)
    return pl.pallas_call(
        hold_kernel,
        out_shape=[jax.ShapeDtypeStruct(x.shape, x.dtype) for x in xs],
        in_specs=[IN_HBM] * (n + len(after)),
        out_specs=[IN_HBM] * n,
        input_output_aliases={i: i for i in range(n)},
        cost_estimate=SHORT,
        name="hold",
    )(*xs, *after)


def finish_kernel(last, blocks, me_ref, *refs):
    out_hbm, out_ref, lines_sum, rows_ref, sem = refs[-5:]
    me, chan, own = me_ref[0], me_ref[1], me_ref[2]
    lags, rows, slots = out_hbm.shape
    pitch = rows + PITCH_PAD
    tiles = slots // LANES
    groups = slots // rows
    taus = lag_rows()
    parts = taus // 8
    base, late, turned = refs[:groups], refs[groups : 2 * groups], refs[2 * groups : 3 * groups]
    scale = [1.0] + [1.0 / F16_SCALE] * (groups - 1)
    lane = lax.broadcasted_iota(jnp.int32, (8, LANES), 1)

    def spread(line, v):
        part = jnp.where(lane < CAP, pltpu.roll(line, LANES - v * CAP, 1), 0.0)
        for shift in (CAP, 2 * CAP, 4 * CAP):
            part = part + pltpu.roll(part, shift, 1)
        return part

    def energy_of(high, low, exponent, e):
        return (high + low) * scale[e] * jnp.exp2(jnp.round(exponent * (64.0 * scale[e])))

    block_of = lax.broadcasted_iota(jnp.int32, (8, slots), 1) // CAP
    every, local = [], []
    for e in range(groups):
        local.append({})
        for n, d in enumerate(last):
            start = (n * parts + parts - 1) * rows
            line = turned[e][start : start + 8]
            local[e][d] = energy_of(spread(line, 6), spread(line, 5), spread(line, 4), e)
        codes = base[e][0, taus - 8 : taus]
        vector = jnp.broadcast_to(energy_of(codes[1:2], codes[2:3], codes[3:4], e), (8, slots))
        for d in last:
            wide = jnp.concatenate([local[e][d]] * tiles, axis=1)
            vector = jnp.where(block_of == jnp.bitwise_xor(me, d), wide, vector)
        every.append(vector)
    norm = lax.rsqrt(sum(every) + 1e-05)
    every = [jnp.sqrt(x) * norm for x in every]
    norms = {d: lax.rsqrt(sum(x[d] for x in local) + 1e-05) for d in last}
    local = [{d: jnp.sqrt(x[d]) * norms[d] for d in last} for x in local]
    for e in range(groups):
        as_rows(every[e] * scale[e], rows_ref.at[e])
    mine = [rows_ref[e, pl.ds(pl.multiple_of(chan * rows, 8), rows), :] for e in range(groups)]
    for n, d in enumerate(last):
        weight = [mine[e] * local[e][d][0:1] for e in range(groups)]
        shift = (jnp.bitwise_xor(me, d) * CAP + LANES - 7 * CAP) % LANES
        for g in range(parts):
            total = 0.0
            for e in range(groups):
                start = (n * parts + g) * rows
                total = total + turned[e][start : start + rows] * weight[e]
            lines_sum[n, g] = pltpu.roll(total, shift, 1)

    def emit(h, from_base):
        d_row = own * blocks + h
        b_row = jnp.bitwise_and(jnp.bitwise_xor(me, d_row), blocks - 1)
        d_late = last[h]

        def one_row(r, carry):
            target = b_row * CAP + r
            slot = jnp.bitwise_xor(me, d_row) * CAP + r
            weight = []
            for e in range(groups):
                row = rows_ref[e, pl.ds(slot, 1), :]
                weight.append(jnp.concatenate([row] * tiles, axis=1) * every[e][0:1])
            for g in range(parts):
                value = 0.0
                for e in range(groups):
                    if from_base:
                        part = base[e][h * CAP + r, 8 * g : 8 * g + 8]
                    else:
                        pieces = []
                        for t in range(tiles):
                            start = pl.multiple_of(((h * tiles + t) * CAP + r) * taus + 8 * g, 8)
                            pieces.append(late[e][pl.ds(start, 8), :])
                        part = jnp.concatenate(pieces, axis=1)
                    value = value + part * weight[e]
                for n, d in enumerate(last):
                    if not from_base and d <= d_late:
                        continue
                    line = jnp.broadcast_to(lines_sum[n, g, pl.ds(target, 1), :], (8, LANES))
                    line = pltpu.roll(line, 0, 1, stride=CAP, stride_axis=0)
                    line = jnp.concatenate([line] * tiles, axis=1)
                    value = jnp.where(block_of == jnp.bitwise_xor(me, d), line, value)
                stop = min(8, lags - 8 * g)
                for t in range(tiles):
                    part = value[:stop, t * LANES : (t + 1) * LANES]
                    if stop < 8:
                        out_ref[t, 8 * g : 8 * g + stop, pl.ds(target, 1), :] = part.reshape(stop, 1, LANES)
                    else:
                        flat = out_ref.at[t].reshape(lags * pitch, LANES)
                        flat[pl.ds(8 * g * pitch + target, stop, stride=pitch), :] = part
            return carry

        lax.fori_loop(0, CAP, one_row, 0, unroll=2)

    @pl.when(own < groups - 1)
    def _():
        for h in range(blocks):
            emit(h, True)

    @pl.when(own == groups - 1)
    def _():
        for h in range(blocks):
            emit(h, False)

    copies = []
    for t in range(tiles):
        target = out_hbm.at[:, :, t * LANES : (t + 1) * LANES]
        copies.append(pltpu.make_async_copy(out_ref.at[t, :, :rows], target, sem.at[t]))
        copies[-1].start()
    for c in copies:
        c.wait()


def finish(me, base, late, turned, last, blocks):
    rows, taus, slots = base[0].shape
    groups = slots // rows
    lags = 2 * MAXLAG + 1
    out = pl.pallas_call(
        functools.partial(finish_kernel, last, blocks),
        out_shape=jax.ShapeDtypeStruct((lags, rows, slots), F32),
        in_specs=[IN_SMEM] + [IN_VMEM] * (3 * groups),
        out_specs=IN_HBM,
        scratch_shapes=[
            pltpu.VMEM((slots // LANES, lags, rows + PITCH_PAD, LANES), F32),
            pltpu.VMEM((len(last), taus // 8, rows, LANES), F32),
            pltpu.VMEM((groups, slots, LANES), F32),
            pltpu.SemaphoreType.DMA((slots // LANES,)),
        ],
        cost_estimate=SHORT,
        compiler_params=pltpu.CompilerParams(vmem_limit_bytes=FINISH_LIMIT),
        name="finish",
    )(me, *base, *late, *turned)
    return jnp.transpose(out, (1, 0, 2))


def local(waveforms, family_of, channel_mask):
    owners = lax.axis_size("fam")
    groups = lax.axis_size("chan")
    blocks = owners // groups
    slots = owners * CAP
    rows = blocks * CAP
    chans, length = waveforms.shape[1:]
    fam = lax.axis_index("fam")
    chan = lax.axis_index("chan")
    own = jnp.bitwise_xor(chan, fam // blocks)
    me = jnp.stack([fam, chan, own, fam // blocks]).astype(jnp.int32)

    half_lanes = LANES // 2
    mask = jnp.pad(channel_mask.astype(F32), ((0, 0), (0, half_lanes - chans)))
    mask = jnp.tile(mask, (1, 4))
    table = jnp.asarray(transform_table(length))
    lags = jnp.asarray(lag_table(length))
    taus = lag_rows()

    half = owners // 2
    last = list(range(owners - blocks, owners))
    early = [d for d in range(owners) if d not in last]
    first = list(range(half, half + blocks))
    sends, inbox = {}, {}
    widen = ((0, 0), (0, half_lanes - chans), (0, 0))

    def collect(dests, after):
        sends.update(zip(dests, gather(me, family_of, waveforms, owners, dests, after)))

    def post(d):
        inbox[d] = jnp.pad(lax.ppermute(sends[d], "fam", [(i, i ^ d) for i in range(owners)]), widen)

    def chan_permute(x, e):
        return lax.ppermute(x, "chan", [(i, i ^ e) for i in range(groups)])

    partners = list(range(groups - 1, 0, -1))

    collect(list(range(half + blocks)), [])
    for d in first + list(range(1, half)):
        post(d)
    inbox[0] = jnp.pad(sends[0], widen)
    ms, energy = whiten({0: inbox[0]}, table, mask, owners, [], [])
    ms, got = whiten({1: inbox[1]}, table, mask, owners, [ms], [])
    energy.update(got)
    remaining = list(range(half + blocks, owners))
    collect(remaining, [got[1]] + [inbox[d] for d in range(1, half)])
    for d in remaining:
        post(d)
    after = [sends[remaining[0]]]
    for start in range(2, half, 4):
        ds = range(start, min(start + 4, half))
        ms, got = whiten({d: inbox[d] for d in ds}, table, mask, owners, [ms], after)
        energy.update(got)
        after = []

    middle = [d for d in early if d >= half]
    limit = max(1, 16 * 2**20 // (CAP * length * slots * 4))
    per_call = max(n for n in range(blocks, len(early) + 1, blocks) if len(early) % n == 0 and n <= max(limit, blocks))
    filled = []
    for start in range(0, len(early), per_call):
        lines_of = early[start : start + per_call]
        xs = {d: inbox[d] for d in middle}
        more = int(start == 0)
        result = square(me, xs, table, mask, lags, ms, energy, lines_of, slots, groups, more, after, filled)
        filled = [result[0]]
        after = [result[1]]
        if more:
            ms = result[-1]

    def narrow(x):
        return (x * F16_SCALE).astype(jnp.float16)

    early_rows = filled[0].reshape(groups, rows * taus, slots)
    sent = {e: chan_permute(narrow(early_rows[e]), e) for e in partners}

    kept = []
    for n, d in enumerate(last):
        result = step(me, inbox[d], table, mask, lags, ms, d, slots, groups, kept, after)
        kept = result[:2]
        after = []
        if n < len(last) - 1:
            ms = result[2]
    late = kept[0]
    (turned,) = hold(kept[1:], [sum(sent[e][:8].astype(F32) for e in partners)])

    def widen_f32(x, shape):
        return x.astype(F32).reshape(shape)

    base_parts, late_parts, turned_parts = [filled[0][0]], [late], [turned[0]]
    small = narrow(late)
    got_late, got_turned = {}, {}
    for e in partners:
        to_owner = []
        for f in range(owners):
            owner = (f // blocks) ^ (groups - 1)
            to_owner.append(((owner ^ e) * owners + f, owner * owners + f))
        got_late[e] = lax.ppermute(small, ("chan", "fam"), to_owner).astype(F32)
        got_turned[e] = chan_permute(narrow(turned[e]), e).astype(F32)
    for e in range(1, groups):
        base_parts.append(widen_f32(sent[e], (rows, taus, slots)))
        late_parts.append(got_late[e])
        turned_parts.append(got_turned[e])
    return finish(me, base_parts, late_parts, turned_parts, last, blocks)[None]


def solution(mesh):
    in_specs = (P("fam", "chan", None), P("fam"), P("fam", "chan"))
    out_specs = P("fam", "chan", None, None)
    return jax.shard_map(local, mesh=mesh, in_specs=in_specs, out_specs=out_specs, check_vma=False)
```

```python
import functools
import math

import jax
import jax.numpy as jnp
import numpy as np
from jax import lax
from jax.experimental import pallas as pl
from jax.experimental.pallas import tpu as pltpu
from jax.sharding import PartitionSpec as P

MAXLAG = 32
LAGS = 2 * MAXLAG + 1
CAP = 16
LANES = 128
F16_SCALE = 16384.0
TINY = 1.2e-38
VMEM_LIMIT = 56 * 2**20
PITCH_PAD = 8
LOAD_PARTS = 1
LONG = pl.CostEstimate(flops=10**14, bytes_accessed=1, transcendentals=0)
SHORT = pl.CostEstimate(flops=1, bytes_accessed=1, transcendentals=0)
FINISH_LIMIT = 40 * 2**20
F32 = jnp.float32
BF16 = jnp.bfloat16
IN_VMEM = pl.BlockSpec(memory_space=pltpu.VMEM)
IN_SMEM = pl.BlockSpec(memory_space=pltpu.SMEM)
IN_HBM = pl.BlockSpec(memory_space=pltpu.HBM)


def split(x):
    high = x.astype(BF16)
    return high, (x - high.astype(F32)).astype(BF16)


def split_table(table):
    high = table.astype(np.float32).astype(BF16)
    return high, (table - high.astype(np.float64)).astype(np.float32).astype(BF16)


def dot(a, b):
    return lax.dot_general(a, b, (((1,), (0,)), ((), ())), preferred_element_type=F32)


def dot_rows(a, b):
    return lax.dot_general(a, b, (((1,), (1,)), ((), ())), preferred_element_type=F32)


def transform_table(length):
    bins = length // 2
    angle = (np.arange(bins)[:, None] * np.arange(length)[None, :] % length) * (2.0 * math.pi / length)
    return np.concatenate(split_table(np.concatenate([np.cos(angle), -np.sin(angle)], axis=0)), axis=0)


def lag_rows():
    return (2 * MAXLAG + 1 + 7) // 8 * 8


def lag_table(length):
    bins = length // 2
    rows = lag_rows()
    shifts = np.arange(rows) - MAXLAG
    angle = (shifts[:, None] * np.arange(bins)[None, :] % length) * (2.0 * math.pi / length)
    table = np.concatenate([np.cos(angle), -np.sin(angle)], axis=1)
    high, low = split_table(table * (shifts <= MAXLAG)[:, None])
    return np.concatenate([high, low], axis=0)


def gather_kernel(owners, dests, me_ref, family_ref, wave_ref, *rest):
    outs = dict(zip(dests, rest[-5 - len(dests) : -5]))
    count, zero, buf, arrived, sent = rest[-5:]
    index = {d: n for n, d in enumerate(dests)}
    me = me_ref[0]
    zero[...] = jnp.zeros_like(zero)
    for f in range(owners):
        count[f] = 0

    def place(e, carry):
        f = family_ref[e]
        r = count[f]
        count[f] = r + 1
        d = jnp.bitwise_xor(f, me)
        spot = jnp.where(r < CAP // 2, 2 * r, 2 * r - CAP + 1)
        slot = d - dests[0]

        @pl.when((d >= dests[0]) & (d <= dests[-1]))
        def _():
            pltpu.make_async_copy(wave_ref.at[e], buf.at[slot, spot], arrived.at[slot]).start()

        return carry

    lax.fori_loop(0, family_ref.shape[0], place, 0, unroll=4)
    for d in dests:

        def fill(r, carry):
            spot = jnp.where(r < CAP // 2, 2 * r, 2 * r - CAP + 1)
            pltpu.make_async_copy(zero, buf.at[index[d], spot], arrived.at[index[d]]).start()
            return carry

        lax.fori_loop(count[jnp.bitwise_xor(me, d)], CAP, fill, 0)
    for d in dests:
        n = index[d]
        pltpu.make_async_copy(buf.at[n], buf.at[n], arrived.at[n]).wait()
        pltpu.make_async_copy(buf.at[n], outs[d], sent.at[n]).start()
    for d in dests:
        n = index[d]
        pltpu.make_async_copy(buf.at[n], outs[d], sent.at[n]).wait()


def gather(me, family_of, waveforms, owners, dests, after):
    shape = (CAP,) + waveforms.shape[1:]
    count = len(dests)
    return pl.pallas_call(
        functools.partial(gather_kernel, owners, dests),
        out_shape=[jax.ShapeDtypeStruct(shape, waveforms.dtype)] * count,
        in_specs=[IN_SMEM, IN_SMEM, IN_HBM] + [IN_HBM] * len(after),
        out_specs=[IN_HBM] * count,
        scratch_shapes=[
            pltpu.SMEM((owners,), jnp.int32),
            pltpu.VMEM(waveforms.shape[1:], waveforms.dtype),
            pltpu.VMEM((count,) + shape, waveforms.dtype),
            pltpu.SemaphoreType.DMA((count,)),
            pltpu.SemaphoreType.DMA((count,)),
        ],
        cost_estimate=SHORT,
        compiler_params=pltpu.CompilerParams(vmem_limit_bytes=VMEM_LIMIT),
        name="gather_slots",
    )(me, family_of, waveforms, *after)


def spot_of(event):
    return event % 2 * (CAP // 2) + event // 2


def code_of(tile):
    exponent = jnp.floor(jnp.log2(jnp.maximum(tile, TINY)))
    mantissa = tile * jnp.exp2(-exponent)
    high = mantissa.astype(BF16).astype(F32)
    return high, mantissa - high, exponent * (1.0 / 64.0)


def whiten_body(x_ref, table_ref, mask_ref, scratch, write):
    events, chans, length = x_ref.shape
    bins = length // 2
    cols = 2 * LANES
    step = cols // chans
    groups = events * chans // LANES
    row = lax.broadcasted_iota(jnp.int32, (bins, cols), 0)
    col = lax.broadcasted_iota(jnp.int32, (bins, cols), 1)
    near = (jnp.abs(row - jnp.bitwise_and(col, bins - 1)) <= 4).astype(F32).astype(BF16)
    count = jnp.minimum(row + 4, bins - 1) - jnp.maximum(row - 4, 0) + 1
    inverse = 1.0 / count.astype(F32)
    row = lax.broadcasted_iota(jnp.int32, (cols, cols), 0) // chans
    col = lax.broadcasted_iota(jnp.int32, (cols, cols), 1) // chans
    same = (row == col).astype(F32).astype(BF16)
    lane = jnp.bitwise_and(lax.broadcasted_iota(jnp.int32, (8, LANES), 1), CAP - 1)
    tile = jnp.zeros((8, LANES), F32)
    for n in range(events // step):
        x = x_ref[n * step : (n + 1) * step].reshape(cols, length)
        spec = dot_rows(table_ref[:length], x) + dot_rows(table_ref[length:], x)
        re = spec[:bins]
        im = spec[bins:]
        power = re * re + im * im
        high, low = split(power)
        smooth = dot(near, jnp.concatenate([high, low], axis=0))
        level = jnp.sum(power, axis=0, keepdims=True) * (0.1 / bins) + 1e-5
        scale = lax.rsqrt(smooth * inverse + level) * mask_ref[...]
        lane_energy = jnp.sum(power * (scale * scale), axis=0, keepdims=True)
        high, low = split(lane_energy)
        rest = (lane_energy - high.astype(F32) - low.astype(F32)).astype(BF16)
        parts = jnp.concatenate([high, low, rest] + [jnp.zeros_like(high)] * 13, axis=0)
        energy = jnp.sum(dot(parts, same), axis=0, keepdims=True)
        for e in range(step):
            value = jnp.broadcast_to(energy[:, e * chans : e * chans + 1], (8, LANES))
            tile = jnp.where(lane == spot_of(n * step + e), value, tile)
        unit = jnp.where(energy > TINY, lax.rsqrt(jnp.maximum(energy, TINY)), 0.0)
        factor = scale * unit
        re = re * factor
        im = im * factor
        for h in range(2):
            g = 2 * n + h
            scratch[g * bins : (g + 1) * bins] = re[:, h * LANES : (h + 1) * LANES]
            scratch[(groups + g) * bins : (groups + g + 1) * bins] = im[:, h * LANES : (h + 1) * LANES]
    first = lax.broadcasted_iota(jnp.int32, (groups, LANES), 1) < LANES // 2

    def relayout(k, carry):
        re = scratch[pl.ds(k, groups, stride=bins), :]
        im = scratch[pl.ds(groups * bins + k, groups, stride=bins), :]
        re_rolled = pltpu.roll(re, LANES // 2, 1)
        im_rolled = pltpu.roll(im, LANES // 2, 1)
        member = jnp.concatenate([jnp.where(first, re, im_rolled), jnp.where(first, re_rolled, im)], axis=0)
        write(k, *split(member))
        return carry

    lax.fori_loop(0, bins, relayout, 0, unroll=32)
    return tile


def whiten_kernel(ds, table_hbm, mask_ref, *refs):
    count = len(ds)
    x_hbm = refs[:count]
    m_hbm, e_ref = refs[-8 - count], refs[-7 - count : -7]
    x_ref, table_ref, m_ref, scratch, sem, x_sem, out_sem = refs[-7:]
    load = pltpu.make_async_copy(table_hbm, table_ref, sem)
    load.start()
    loads = [pltpu.make_async_copy(x_hbm[n], x_ref.at[n], x_sem.at[n]) for n in range(count)]
    for c in loads:
        c.start()
    load.wait()
    outs = []
    for n, d in enumerate(ds):
        loads[n].wait()

        def write(k, high, low):
            m_ref[n, k, :, :LANES] = high
            m_ref[n, k, :, LANES:] = low

        e_ref[n][...] = whiten_body(x_ref.at[n], table_ref, mask_ref, scratch.at[n % 2], write)
        outs.append(pltpu.make_async_copy(m_ref.at[n], m_hbm.at[d], out_sem.at[n]))
        outs[-1].start()
    for c in outs:
        c.wait()


def member_shapes(x):
    events, chans, length = x.shape
    bins = length // 2
    m = jax.ShapeDtypeStruct((bins, events, 2 * LANES), BF16)
    return m, (2 * events * chans // LANES * bins, LANES)


ENERGY = jax.ShapeDtypeStruct((8, LANES), F32)


def whiten(xs, table, mask, owners, filled, after):
    ds = sorted(xs)
    count = len(ds)
    m, scratch = member_shapes(xs[ds[0]])
    out = pl.pallas_call(
        functools.partial(whiten_kernel, ds),
        out_shape=[jax.ShapeDtypeStruct((owners,) + m.shape, m.dtype)] + [ENERGY] * count,
        in_specs=[IN_HBM, IN_VMEM] + [IN_HBM] * (count + len(after) + len(filled)),
        out_specs=[IN_HBM] + [IN_VMEM] * count,
        scratch_shapes=[
            pltpu.VMEM((count,) + xs[ds[0]].shape, xs[ds[0]].dtype),
            pltpu.VMEM(table.shape, table.dtype),
            pltpu.VMEM((count,) + m.shape, m.dtype),
            pltpu.VMEM((2,) + scratch, F32),
            pltpu.SemaphoreType.DMA,
            pltpu.SemaphoreType.DMA((count,)),
            pltpu.SemaphoreType.DMA((count,)),
        ],
        cost_estimate=SHORT,
        input_output_aliases={2 + count + len(after): 0} if filled else {},
        compiler_params=pltpu.CompilerParams(vmem_limit_bytes=VMEM_LIMIT),
        name="whiten",
    )(table, mask, *[xs[d] for d in ds], *after, *filled)
    return out[0], dict(zip(ds, out[1:]))


def turn(m):
    half = LANES // 2
    return jnp.concatenate([m[:, half:LANES], -m[:, :half]], axis=1)


def pairs_body(me, new, members, table_ref, cross_ref, copies, emit, ready):
    count, bins, _, _ = members.shape
    slots = count * CAP
    tiles = slots // LANES
    taus = table_ref.shape[0] // 2
    n = len(new) * CAP
    pitch = 2 * bins + PITCH_PAD

    def cross(k, carry):
        both = jnp.concatenate([members[jnp.bitwise_xor(me, b), k] for b in range(count)], axis=0)
        left = jnp.concatenate([members[d, k] for d in new], axis=0)
        high = left[:, :LANES]
        low = left[:, LANES:]
        left = jnp.concatenate([high, turn(high), low, turn(low)], axis=0)
        right = jnp.concatenate([both[:, :LANES], both[:, LANES:]], axis=0)
        if n <= 32:
            out = dot_rows(left, right)
            total = out[: 2 * n, :slots] + (out[: 2 * n, slots:] + out[2 * n :, :slots])
        else:
            out = dot_rows(left[: 2 * n], right)
            total = out[:, :slots] + (out[:, slots:] + dot_rows(left[2 * n :], right[:slots]))
        for q in range(2):
            for t in range(tiles):
                part = total[q * n : (q + 1) * n, t * LANES : (t + 1) * LANES]
                cross_ref[t, pl.ds(q * bins + k, n, stride=pitch), :] = part
        return carry

    step = bins // LOAD_PARTS
    for p in range(LOAD_PARTS):
        copies[p].wait()
        lax.fori_loop(p * step, (p + 1) * step, cross, 0, unroll=32 if n <= 32 else 16)
    table = table_ref[...]

    def lag(i, carry):
        for t in range(tiles):
            pair = cross_ref[t, pl.ds(pl.multiple_of(2 * i * pitch, 8), 2 * pitch), :]
            pair = jnp.concatenate([pair[: 2 * bins], pair[pitch : pitch + 2 * bins]], axis=1)
            high, low = split(pair)
            out = dot(table, high)
            out = out[:taus] + (out[taus:] + dot(table[:taus], low))
            for h in range(2):
                emit(2 * i + h, t, out[:, h * LANES : (h + 1) * LANES])
        return carry

    for start in range(0, n // 2, CAP):
        stop = min(start + CAP, n // 2)
        lax.fori_loop(start, stop, lag, 0, unroll=8)
        ready(2 * stop)


def turn_lines(lines, codes, chan, turned, taus):
    tiles = lines.shape[0] // (CAP * LAGS)
    groups, parts = turned.shape[0], taus // 8
    rows = turned.shape[1] // parts
    for g in range(parts):
        for t in range(tiles):
            pieces = []
            for u in range(7, -1, -1):
                tau = 2 * MAXLAG - 8 * g - u
                if tau >= 0:
                    pieces.append(lines[pl.ds(t * CAP * LAGS + tau, CAP, stride=LAGS), :])
                else:
                    pieces.append(codes[min(-tau, len(codes)) - 1])
            value = jnp.concatenate(pieces, axis=0).T
            for c in range(LANES // rows):
                target = jnp.bitwise_xor(chan, t * (LANES // rows) + c)
                turned[target, g * rows : (g + 1) * rows] = value[c * rows : (c + 1) * rows]


def place(me, d):
    return pl.multiple_of(jnp.bitwise_xor(me, d) * CAP, CAP)


def load_members(m_hbm, count, members, sem):
    step = members.shape[1] // LOAD_PARTS
    copies = []
    for p in range(LOAD_PARTS):
        part = pl.ds(p * step, step)
        source, target = m_hbm.at[pl.ds(0, count), part], members.at[pl.ds(0, count), part]
        copies.append(pltpu.make_async_copy(source, target, sem.at[p]))
        copies[-1].start()
    return copies


def slot_vector(me, tiles, slots):
    lane = lax.broadcasted_iota(jnp.int32, (8, slots), 1) // CAP
    value = jnp.zeros((8, slots), F32)
    for d, tile in tiles.items():
        value = jnp.where(lane == jnp.bitwise_xor(me, d), jnp.concatenate([tile] * (slots // LANES), axis=1), value)
    return value


def as_rows(value, ref):
    for t in range(value.shape[1] // LANES):
        part = jnp.broadcast_to(value[0:1, t * LANES : (t + 1) * LANES], (LANES, LANES))
        ref[t * LANES : (t + 1) * LANES] = part.T


def whiten_and_load(new, count, me, x_hbm, m_hbm, tables, buffers, sems, keep):
    table_hbm, mask_ref = tables
    x_ref, table_ref, scratch, members = buffers
    load, x_sem, sem = sems
    table_load = pltpu.make_async_copy(table_hbm, table_ref, load)
    table_load.start()
    loads = [pltpu.make_async_copy(x_hbm[n], x_ref.at[n], x_sem.at[n]) for n in range(len(new))]
    for c in loads:
        c.start()
    copies = load_members(m_hbm, count, members, sem)
    table_load.wait()
    tiles = {}
    for n, d in enumerate(new):
        loads[n].wait()

        def write(k, high, low):
            members[d, k, :, :LANES] = high
            members[d, k, :, LANES:] = low

        tiles[d] = whiten_body(x_ref.at[n], table_ref, mask_ref, scratch.at[n % 2], write)
        keep(d, members.at[d])
    return tiles, copies


def shared_scratch(x, new, table, slots, n):
    m, scratch = member_shapes(x)
    bins = m.shape[0]
    return [
        pltpu.VMEM((len(new),) + x.shape, x.dtype),
        pltpu.VMEM(table.shape, table.dtype),
        pltpu.VMEM((min(2, len(new)),) + scratch, F32),
        pltpu.VMEM((slots // CAP, bins, CAP, 2 * LANES), BF16),
        pltpu.VMEM((slots // LANES, n * (2 * bins + PITCH_PAD), LANES), F32),
        pltpu.SemaphoreType.DMA,
        pltpu.SemaphoreType.DMA((len(new),)),
        pltpu.SemaphoreType.DMA((LOAD_PARTS,)),
        pltpu.SemaphoreType.DMA((24,)),
    ]


def square_kernel(old, new, lines_of, more, me_ref, table_hbm, mask_ref, lag_ref, *refs):
    count = len(new)
    x_hbm, refs = refs[:count], refs[count:]
    m_hbm, refs = refs[0], refs[1:]
    given, refs = refs[: len(old)], refs[len(old) :]
    x_ref, table_ref, scratch, members, cross_ref, load, x_sem, sem, out_sem, rows_ref = refs[-10:]
    outs = refs[-10 - 1 - count - more : -10]
    me, own = me_ref[0], me_ref[2]
    slots = members.shape[0] * CAP
    done = []

    def keep(d, block):
        if more:
            done.append(pltpu.make_async_copy(block, outs[1 + count].at[d], out_sem.at[8 + len(done)]))
            done[-1].start()

    buffers = (x_ref, table_ref, scratch, members)
    sems = (load, x_sem, sem)
    tables = (table_hbm, mask_ref)
    tiles, copies = whiten_and_load(new, len(old), me, x_hbm, m_hbm, tables, buffers, sems, keep)
    for n, d in enumerate(new):
        outs[1 + n][...] = tiles[d]
    for d, ref in zip(old, given):
        tiles[d] = ref[...]
    codes = code_of(slot_vector(me, tiles, slots))

    def emit(row, t, part):
        rows_ref[row, :, t * LANES : (t + 1) * LANES] = part

    groups, rows = outs[0].shape[:2]
    first = lines_of[0] * CAP // rows

    def ready(stop):
        if stop % rows == 0:
            n = stop // rows - 1
            for c, code in enumerate(codes):
                rows_ref[n * rows, 2 * MAXLAG + 1 + c : 2 * MAXLAG + 2 + c] = code[0:1]
            target = jnp.bitwise_xor(first + n, own)
            part = rows_ref.at[n * rows : (n + 1) * rows]
            done.append(pltpu.make_async_copy(part, outs[0].at[target], out_sem.at[n]))
            done[-1].start()

    pairs_body(me, lines_of, members, lag_ref, cross_ref, copies, emit, ready)
    if first + rows_ref.shape[0] // rows == groups - 1:
        target = jnp.bitwise_xor(groups - 1, own)
        done.append(pltpu.make_async_copy(rows_ref.at[:rows], outs[0].at[target], out_sem.at[groups - 1]))
        done[-1].start()
    for c in done:
        c.wait()


def square(me, xs, table, mask, lags, ms, energy, lines_of, slots, groups, more, after, filled):
    old, new = sorted(energy), sorted(xs)
    taus = lags.shape[0] // 2
    x = xs[new[0]]
    n = len(lines_of) * CAP
    rows = jax.ShapeDtypeStruct((groups, slots // groups, taus, slots), F32)
    members = jax.ShapeDtypeStruct(ms.shape, ms.dtype)
    aliases = {4 + len(new): 1 + len(new)} if more else {}
    if filled:
        aliases[5 + len(new) + len(old) + len(after)] = 0
    return pl.pallas_call(
        functools.partial(square_kernel, old, new, lines_of, more),
        out_shape=[rows] + [ENERGY] * len(new) + [members] * more,
        in_specs=[IN_SMEM, IN_HBM, IN_VMEM, IN_VMEM]
        + [IN_HBM] * (len(new) + 1)
        + [IN_VMEM] * len(old)
        + [IN_HBM] * (len(after) + len(filled)),
        out_specs=[IN_HBM] + [IN_VMEM] * len(new) + [IN_HBM] * more,
        scratch_shapes=shared_scratch(x, new, table, slots, n) + [pltpu.VMEM((n, taus, slots), F32)],
        cost_estimate=SHORT,
        input_output_aliases=aliases,
        compiler_params=pltpu.CompilerParams(vmem_limit_bytes=VMEM_LIMIT),
        name="square",
    )(me, table, mask, lags, *[xs[d] for d in new], ms, *[energy[d] for d in old], *after, *filled)


def step_kernel(new, final, me_ref, table_hbm, mask_ref, lag_ref, x_hbm, m_hbm, *refs):
    lines, turned_ref = refs[-2:]
    x_ref, table_ref, scratch, members, cross_ref, load, x_sem, sem, out_sem = refs[-11:-2]
    outs = refs[-11 - (2 if final else 4) : -11]
    me, chan = me_ref[0], me_ref[1]
    slots = members.shape[0] * CAP
    taus = lag_ref.shape[0] // 2
    done = []

    def start(source, target):
        done.append(pltpu.make_async_copy(source, target, out_sem.at[len(done)]))
        done[-1].start()

    def keep(d, block):
        if not final:
            start(block, outs[2].at[d])

    full_turned = turned_ref
    if final:
        kept_turned = refs[0]
        turned_cut = kept_turned.shape[1]
        start(kept_turned, turned_ref.at[:, :turned_cut])
        turned_ref = turned_ref.at[:, turned_cut:]
    buffers = (x_ref, table_ref, scratch, members)
    sems = (load, x_sem, sem)
    tiles, copies = whiten_and_load([new], new, me, [x_hbm], m_hbm, (table_hbm, mask_ref), buffers, sems, keep)
    tile = tiles[new]
    column = jnp.broadcast_to(tile[0:1], (LANES, LANES)).T[:CAP]

    def emit(row, t, part):
        lines[pl.ds((t * CAP + row) * LAGS, LAGS), :] = part[:LAGS]

    pairs_body(me, [new], members, lag_ref, cross_ref, copies, emit, lambda stop: None)
    if final:
        for c in done:
            c.wait()
    else:
        outs[3][...] = tile
    start(lines, outs[0])
    turn_lines(lines, code_of(column), chan, turned_ref, taus)
    start(full_turned, outs[1])
    for c in done[1:] if final else done:
        c.wait()


def step(me, x, table, mask, lags, ms, new, slots, groups, kept, after):
    taus = lags.shape[0] // 2
    final = len(kept) > 0
    parts = taus // 8 * (slots // groups)
    lines = jax.ShapeDtypeStruct((slots // LANES * CAP * LAGS, LANES), F32)
    turned = jax.ShapeDtypeStruct((groups, parts + (kept[0].shape[1] if final else 0), LANES), F32)
    members = jax.ShapeDtypeStruct(ms.shape, ms.dtype)
    return pl.pallas_call(
        functools.partial(step_kernel, new, final),
        out_shape=[lines, turned] + ([] if final else [members, ENERGY]),
        in_specs=[IN_SMEM, IN_HBM, IN_VMEM, IN_VMEM] + [IN_HBM] * (2 + len(kept) + len(after)),
        out_specs=[IN_HBM] * 2 + ([] if final else [IN_HBM, IN_VMEM]),
        scratch_shapes=shared_scratch(x, [new], table, slots, CAP)
        + [pltpu.VMEM(lines.shape, F32), pltpu.VMEM(turned.shape, F32)],
        cost_estimate=LONG if final else SHORT,
        input_output_aliases={} if final else {5: 2},
        compiler_params=pltpu.CompilerParams(vmem_limit_bytes=VMEM_LIMIT),
        name="step",
    )(me, table, mask, lags, x, ms, *kept, *after)


def hold_kernel(*refs):
    del refs


def hold(xs, after):
    n = len(xs)
    return pl.pallas_call(
        hold_kernel,
        out_shape=[jax.ShapeDtypeStruct(x.shape, x.dtype) for x in xs],
        in_specs=[IN_HBM] * (n + len(after)),
        out_specs=[IN_HBM] * n,
        input_output_aliases={i: i for i in range(n)},
        cost_estimate=SHORT,
        name="hold",
    )(*xs, *after)


def finish_kernel(last, blocks, me_ref, *refs):
    out_hbm, out_ref, lines_sum, rows_ref, sem = refs[-5:]
    me, chan, own = me_ref[0], me_ref[1], me_ref[2]
    lags, rows, slots = out_hbm.shape
    pitch = rows + PITCH_PAD
    tiles = slots // LANES
    groups = slots // rows
    taus = lag_rows()
    parts = taus // 8
    base, turned = refs[:groups], refs[groups : 2 * groups]
    late = [refs[(2 + n) * groups : (3 + n) * groups] for n in range(len(last))]
    scale = [1.0] + [1.0 / F16_SCALE] * (groups - 1)
    lane = lax.broadcasted_iota(jnp.int32, (8, LANES), 1)

    def spread(line, v):
        part = jnp.where(lane < CAP, pltpu.roll(line, LANES - v * CAP, 1), 0.0)
        for shift in (CAP, 2 * CAP, 4 * CAP):
            part = part + pltpu.roll(part, shift, 1)
        return part

    def energy_of(high, low, exponent, e):
        return (high + low) * scale[e] * jnp.exp2(jnp.round(exponent * (64.0 * scale[e])))

    block_of = lax.broadcasted_iota(jnp.int32, (8, slots), 1) // CAP
    every, local = [], []
    for e in range(groups):
        local.append({})
        for n, d in enumerate(last):
            start = (n * parts + parts - 1) * rows
            line = turned[e][start : start + 8]
            local[e][d] = energy_of(spread(line, 6), spread(line, 5), spread(line, 4), e)
        codes = base[e][0, taus - 8 : taus]
        vector = jnp.broadcast_to(energy_of(codes[1:2], codes[2:3], codes[3:4], e), (8, slots))
        for d in last:
            wide = jnp.concatenate([local[e][d]] * tiles, axis=1)
            vector = jnp.where(block_of == jnp.bitwise_xor(me, d), wide, vector)
        every.append(vector)
    norm = lax.rsqrt(sum(every) + 1e-05)
    every = [jnp.sqrt(x) * norm for x in every]
    norms = {d: lax.rsqrt(sum(x[d] for x in local) + 1e-05) for d in last}
    local = [{d: jnp.sqrt(x[d]) * norms[d] for d in last} for x in local]
    for e in range(groups):
        as_rows(every[e] * scale[e], rows_ref.at[e])
    mine = [rows_ref[e, pl.ds(pl.multiple_of(chan * rows, 8), rows), :] for e in range(groups)]
    for n, d in enumerate(last):
        weight = [mine[e] * local[e][d][0:1] for e in range(groups)]
        shift = (jnp.bitwise_xor(me, d) * CAP + LANES - 7 * CAP) % LANES
        for g in range(parts):
            total = 0.0
            for e in range(groups):
                start = (n * parts + g) * rows
                total = total + turned[e][start : start + rows] * weight[e]
            lines_sum[n, g] = pltpu.roll(total, shift, 1)

    def emit(h, from_base):
        d_row = own * blocks + h
        b_row = jnp.bitwise_and(jnp.bitwise_xor(me, d_row), blocks - 1)
        d_late = last[h]

        def one_row(r, carry):
            target = b_row * CAP + r
            slot = jnp.bitwise_xor(me, d_row) * CAP + r
            weight = []
            for e in range(groups):
                row = rows_ref[e, pl.ds(slot, 1), :]
                weight.append(jnp.concatenate([row] * tiles, axis=1) * every[e])
            for g in range(parts):
                stop = min(8, lags - 8 * g)
                value = 0.0
                for e in range(groups):
                    if from_base:
                        part = base[e][h * CAP + r, 8 * g : 8 * g + stop]
                    else:
                        pieces = [late[h][e][pl.ds((t * CAP + r) * LAGS + 8 * g, stop), :] for t in range(tiles)]
                        part = jnp.concatenate(pieces, axis=1)
                    value = value + part * weight[e][:stop]
                for n, d in enumerate(last):
                    if not from_base and d <= d_late:
                        continue
                    line = jnp.broadcast_to(lines_sum[n, g, pl.ds(target, 1), :], (8, LANES))
                    line = pltpu.roll(line, 0, 1, stride=CAP, stride_axis=0)[:stop]
                    line = jnp.concatenate([line] * tiles, axis=1)
                    value = jnp.where(block_of[:stop] == jnp.bitwise_xor(me, d), line, value)
                for t in range(tiles):
                    part = value[:, t * LANES : (t + 1) * LANES]
                    if stop < 8:
                        out_ref[t, 8 * g : 8 * g + stop, pl.ds(target, 1), :] = part.reshape(stop, 1, LANES)
                    else:
                        flat = out_ref.at[t].reshape(lags * pitch, LANES)
                        flat[pl.ds(8 * g * pitch + target, stop, stride=pitch), :] = part
            return carry

        lax.fori_loop(0, CAP, one_row, 0, unroll=2)

    @pl.when(own < groups - 1)
    def _():
        for h in range(blocks):
            emit(h, True)

    @pl.when(own == groups - 1)
    def _():
        for h in range(blocks):
            emit(h, False)

    copies = []
    for t in range(tiles):
        target = out_hbm.at[:, :, t * LANES : (t + 1) * LANES]
        copies.append(pltpu.make_async_copy(out_ref.at[t, :, :rows], target, sem.at[t]))
        copies[-1].start()
    for c in copies:
        c.wait()


def finish(me, base, turned, late, last, blocks):
    rows, taus, slots = base[0].shape
    groups = slots // rows
    lags = 2 * MAXLAG + 1
    out = pl.pallas_call(
        functools.partial(finish_kernel, last, blocks),
        out_shape=jax.ShapeDtypeStruct((lags, rows, slots), F32),
        in_specs=[IN_SMEM] + [IN_VMEM] * ((2 + len(last)) * groups),
        out_specs=IN_HBM,
        scratch_shapes=[
            pltpu.VMEM((slots // LANES, lags, rows + PITCH_PAD, LANES), F32),
            pltpu.VMEM((len(last), taus // 8, rows, LANES), F32),
            pltpu.VMEM((groups, slots, LANES), F32),
            pltpu.SemaphoreType.DMA((slots // LANES,)),
        ],
        cost_estimate=SHORT,
        compiler_params=pltpu.CompilerParams(vmem_limit_bytes=FINISH_LIMIT),
        name="finish",
    )(me, *base, *turned, *[x for rows_of in late for x in rows_of])
    return jnp.transpose(out, (1, 0, 2))


def local(waveforms, family_of, channel_mask):
    owners = lax.axis_size("fam")
    groups = lax.axis_size("chan")
    blocks = owners // groups
    slots = owners * CAP
    rows = blocks * CAP
    chans, length = waveforms.shape[1:]
    fam = lax.axis_index("fam")
    chan = lax.axis_index("chan")
    own = jnp.bitwise_xor(chan, fam // blocks)
    me = jnp.stack([fam, chan, own, fam // blocks]).astype(jnp.int32)

    half_lanes = LANES // 2
    mask = jnp.pad(channel_mask.astype(F32), ((0, 0), (0, half_lanes - chans)))
    mask = jnp.tile(mask, (1, 4))
    table = jnp.asarray(transform_table(length))
    lags = jnp.asarray(lag_table(length))
    taus = lag_rows()

    half = owners // 2
    last = list(range(owners - blocks, owners))
    early = [d for d in range(owners) if d not in last]
    first = list(range(half, half + blocks))
    sends, inbox = {}, {}
    widen = ((0, 0), (0, half_lanes - chans), (0, 0))

    def collect(dests, after):
        sends.update(zip(dests, gather(me, family_of, waveforms, owners, dests, after)))

    def post(d):
        inbox[d] = jnp.pad(lax.ppermute(sends[d], "fam", [(i, i ^ d) for i in range(owners)]), widen)

    def chan_permute(x, e):
        return lax.ppermute(x, "chan", [(i, i ^ e) for i in range(groups)])

    partners = list(range(groups - 1, 0, -1))

    collect(list(range(half + blocks)), [])
    for d in first + list(range(1, half)):
        post(d)
    inbox[0] = jnp.pad(sends[0], widen)
    ms, energy = whiten({0: inbox[0]}, table, mask, owners, [], [])
    ms, got = whiten({1: inbox[1]}, table, mask, owners, [ms], [])
    energy.update(got)
    remaining = list(range(half + blocks, owners))
    collect(remaining, [got[1]] + [inbox[d] for d in range(1, half)])
    for d in remaining:
        post(d)
    after = [sends[remaining[0]]]
    for start in range(2, half, 4):
        ds = range(start, min(start + 4, half))
        ms, got = whiten({d: inbox[d] for d in ds}, table, mask, owners, [ms], after)
        energy.update(got)
        after = []

    middle = [d for d in early if d >= half]
    limit = max(1, 16 * 2**20 // (CAP * length * slots * 4))
    per_call = max(n for n in range(blocks, len(early) + 1, blocks) if len(early) % n == 0 and n <= max(limit, blocks))
    filled = []
    for start in range(0, len(early), per_call):
        lines_of = early[start : start + per_call]
        xs = {d: inbox[d] for d in middle}
        more = int(start == 0)
        result = square(me, xs, table, mask, lags, ms, energy, lines_of, slots, groups, more, after, filled)
        filled = [result[0]]
        after = [result[1]]
        if more:
            ms = result[-1]

    def narrow(x):
        return (x * F16_SCALE).astype(jnp.float16)

    early_rows = filled[0].reshape(groups, rows * taus, slots)
    sent = {e: chan_permute(narrow(early_rows[e]), e) for e in partners}

    def to_owner(x, e):
        moves = []
        for f in range(owners):
            owner = (f // blocks) ^ (groups - 1)
            moves.append(((owner ^ e) * owners + f, owner * owners + f))
        return lax.ppermute(x, ("chan", "fam"), moves)

    kept, late = [], []
    for n, d in enumerate(last):
        result = step(me, inbox[d], table, mask, lags, ms, d, slots, groups, kept, after)
        kept, after = [result[1]], []
        small = narrow(result[0])
        late.append([result[0]] + [to_owner(small, e) for e in range(1, groups)])
        if n < len(last) - 1:
            ms = result[2]
    there = [sent[e] for e in partners] + [x for rows_of in late[:-1] for x in rows_of[1:]]
    (turned,) = hold(kept, [sum(x[:8, :LANES].astype(F32) for x in there)])

    base_parts, turned_parts = [filled[0][0]], [turned[0]]
    for e in range(1, groups):
        base_parts.append(sent[e].astype(F32).reshape(rows, taus, slots))
        turned_parts.append(chan_permute(narrow(turned[e]), e).astype(F32))
    late = [[x.astype(F32) for x in rows_of] for rows_of in late]
    return finish(me, base_parts, turned_parts, late, last, blocks)[None]


def solution(mesh):
    in_specs = (P("fam", "chan", None), P("fam"), P("fam", "chan"))
    out_specs = P("fam", "chan", None, None)
    return jax.shard_map(local, mesh=mesh, in_specs=in_specs, out_specs=out_specs, check_vma=False)
```

```python
import functools
import math

import jax
import jax.numpy as jnp
import numpy as np
from jax import lax
from jax.experimental import pallas as pl
from jax.experimental.pallas import tpu as pltpu
from jax.sharding import PartitionSpec as P

MAXLAG = 32
LAGS = 2 * MAXLAG + 1
CAP = 16
LANES = 128
F16_SCALE = 16384.0
TINY = 1.2e-38
VMEM_LIMIT = 56 * 2**20
VMEM_MARGIN = 8 * 2**20
PITCH_PAD = 8
LOAD_PARTS = 1
LONG = pl.CostEstimate(flops=10**14, bytes_accessed=1, transcendentals=0)
SHORT = pl.CostEstimate(flops=1, bytes_accessed=1, transcendentals=0)
FINISH_LIMIT = 40 * 2**20
F32 = jnp.float32
BF16 = jnp.bfloat16
IN_VMEM = pl.BlockSpec(memory_space=pltpu.VMEM)
IN_SMEM = pl.BlockSpec(memory_space=pltpu.SMEM)
IN_HBM = pl.BlockSpec(memory_space=pltpu.HBM)


def room(scratch_shapes):
    buffers = [x for x in scratch_shapes if getattr(x, "memory_space", None) == pltpu.VMEM]
    total = sum(math.prod(x.shape) * jnp.dtype(x.dtype).itemsize for x in buffers)
    return pltpu.CompilerParams(vmem_limit_bytes=min(VMEM_LIMIT, total + VMEM_MARGIN))


def split(x):
    high = x.astype(BF16)
    return high, (x - high.astype(F32)).astype(BF16)


def split_table(table):
    high = table.astype(np.float32).astype(BF16)
    return high, (table - high.astype(np.float64)).astype(np.float32).astype(BF16)


def dot(a, b):
    return lax.dot_general(a, b, (((1,), (0,)), ((), ())), preferred_element_type=F32)


def dot_rows(a, b):
    return lax.dot_general(a, b, (((1,), (1,)), ((), ())), preferred_element_type=F32)


def transform_table(length):
    bins = length // 2
    angle = (np.arange(bins)[:, None] * np.arange(length)[None, :] % length) * (2.0 * math.pi / length)
    return np.concatenate(split_table(np.concatenate([np.cos(angle), -np.sin(angle)], axis=0)), axis=0)


def lag_rows():
    return (2 * MAXLAG + 1 + 7) // 8 * 8


def lag_table(length):
    bins = length // 2
    rows = lag_rows()
    shifts = np.arange(rows) - MAXLAG
    angle = (shifts[:, None] * np.arange(bins)[None, :] % length) * (2.0 * math.pi / length)
    table = np.concatenate([np.cos(angle), -np.sin(angle)], axis=1)
    high, low = split_table(table * (shifts <= MAXLAG)[:, None])
    return np.concatenate([high, low], axis=0)


def gather_kernel(owners, dests, me_ref, family_ref, wave_ref, *rest):
    outs = dict(zip(dests, rest[-5 - len(dests) : -5]))
    count, zero, buf, arrived, sent = rest[-5:]
    index = {d: n for n, d in enumerate(dests)}
    me = me_ref[0]
    zero[...] = jnp.zeros_like(zero)
    for f in range(owners):
        count[f] = 0

    def place(e, carry):
        f = family_ref[e]
        r = count[f]
        count[f] = r + 1
        d = jnp.bitwise_xor(f, me)
        spot = jnp.where(r < CAP // 2, 2 * r, 2 * r - CAP + 1)
        slot = d - dests[0]

        @pl.when((d >= dests[0]) & (d <= dests[-1]))
        def _():
            pltpu.make_async_copy(wave_ref.at[e], buf.at[slot, spot], arrived.at[slot]).start()

        return carry

    lax.fori_loop(0, family_ref.shape[0], place, 0, unroll=4)
    for d in dests:

        def fill(r, carry):
            spot = jnp.where(r < CAP // 2, 2 * r, 2 * r - CAP + 1)
            pltpu.make_async_copy(zero, buf.at[index[d], spot], arrived.at[index[d]]).start()
            return carry

        lax.fori_loop(count[jnp.bitwise_xor(me, d)], CAP, fill, 0)
    for d in dests:
        n = index[d]
        pltpu.make_async_copy(buf.at[n], buf.at[n], arrived.at[n]).wait()
        pltpu.make_async_copy(buf.at[n], outs[d], sent.at[n]).start()
    for d in dests:
        n = index[d]
        pltpu.make_async_copy(buf.at[n], outs[d], sent.at[n]).wait()


def gather(me, family_of, waveforms, owners, dests, after):
    shape = (CAP,) + waveforms.shape[1:]
    count = len(dests)
    return pl.pallas_call(
        functools.partial(gather_kernel, owners, dests),
        out_shape=[jax.ShapeDtypeStruct(shape, waveforms.dtype)] * count,
        in_specs=[IN_SMEM, IN_SMEM, IN_HBM] + [IN_VMEM] * len(after),
        out_specs=[IN_HBM] * count,
        scratch_shapes=[
            pltpu.SMEM((owners,), jnp.int32),
            pltpu.VMEM(waveforms.shape[1:], waveforms.dtype),
            pltpu.VMEM((count,) + shape, waveforms.dtype),
            pltpu.SemaphoreType.DMA((count,)),
            pltpu.SemaphoreType.DMA((count,)),
        ],
        cost_estimate=SHORT,
        compiler_params=pltpu.CompilerParams(vmem_limit_bytes=2 * VMEM_MARGIN if after else VMEM_LIMIT),
        name="gather_slots",
    )(me, family_of, waveforms, *after)


def spot_of(event):
    return event % 2 * (CAP // 2) + event // 2


def code_of(tile):
    exponent = jnp.floor(jnp.log2(jnp.maximum(tile, TINY)))
    mantissa = tile * jnp.exp2(-exponent)
    high = mantissa.astype(BF16).astype(F32)
    return high, mantissa - high, exponent * (1.0 / 64.0)


def whiten_body(x_ref, table_ref, mask_ref, scratch, write):
    events, chans, length = x_ref.shape
    bins = length // 2
    cols = 2 * LANES
    step = cols // chans
    groups = events * chans // LANES
    row = lax.broadcasted_iota(jnp.int32, (bins, cols), 0)
    col = lax.broadcasted_iota(jnp.int32, (bins, cols), 1)
    near = (jnp.abs(row - jnp.bitwise_and(col, bins - 1)) <= 4).astype(F32).astype(BF16)
    count = jnp.minimum(row + 4, bins - 1) - jnp.maximum(row - 4, 0) + 1
    inverse = 1.0 / count.astype(F32)
    row = lax.broadcasted_iota(jnp.int32, (cols, cols), 0) // chans
    col = lax.broadcasted_iota(jnp.int32, (cols, cols), 1) // chans
    same = (row == col).astype(F32).astype(BF16)
    lane = jnp.bitwise_and(lax.broadcasted_iota(jnp.int32, (8, LANES), 1), CAP - 1)
    tile = jnp.zeros((8, LANES), F32)
    for n in range(events // step):
        x = x_ref[n * step : (n + 1) * step].reshape(cols, length)
        spec = dot_rows(table_ref[:length], x) + dot_rows(table_ref[length:], x)
        re = spec[:bins]
        im = spec[bins:]
        power = re * re + im * im
        high, low = split(power)
        smooth = dot(near, jnp.concatenate([high, low], axis=0))
        level = jnp.sum(power, axis=0, keepdims=True) * (0.1 / bins) + 1e-5
        scale = lax.rsqrt(smooth * inverse + level) * mask_ref[...]
        lane_energy = jnp.sum(power * (scale * scale), axis=0, keepdims=True)
        high, low = split(lane_energy)
        rest = (lane_energy - high.astype(F32) - low.astype(F32)).astype(BF16)
        parts = jnp.concatenate([high, low, rest] + [jnp.zeros_like(high)] * 13, axis=0)
        energy = jnp.sum(dot(parts, same), axis=0, keepdims=True)
        for e in range(step):
            value = jnp.broadcast_to(energy[:, e * chans : e * chans + 1], (8, LANES))
            tile = jnp.where(lane == spot_of(n * step + e), value, tile)
        unit = jnp.where(energy > TINY, lax.rsqrt(jnp.maximum(energy, TINY)), 0.0)
        factor = scale * unit
        re = re * factor
        im = im * factor
        for h in range(2):
            g = 2 * n + h
            scratch[g * bins : (g + 1) * bins] = re[:, h * LANES : (h + 1) * LANES]
            scratch[(groups + g) * bins : (groups + g + 1) * bins] = im[:, h * LANES : (h + 1) * LANES]
    first = lax.broadcasted_iota(jnp.int32, (groups, LANES), 1) < LANES // 2

    def relayout(k, carry):
        re = scratch[pl.ds(k, groups, stride=bins), :]
        im = scratch[pl.ds(groups * bins + k, groups, stride=bins), :]
        re_rolled = pltpu.roll(re, LANES // 2, 1)
        im_rolled = pltpu.roll(im, LANES // 2, 1)
        member = jnp.concatenate([jnp.where(first, re, im_rolled), jnp.where(first, re_rolled, im)], axis=0)
        write(k, *split(member))
        return carry

    lax.fori_loop(0, bins, relayout, 0, unroll=32)
    return tile


def whiten_kernel(ds, table_hbm, mask_ref, *refs):
    count = len(ds)
    x_refs = refs[:count]
    m_hbm, e_ref = refs[-6 - count], refs[-5 - count : -5]
    table_ref, m_ref, scratch, sem, out_sem = refs[-5:]
    load = pltpu.make_async_copy(table_hbm, table_ref, sem)
    load.start()
    load.wait()
    outs = []
    for n, d in enumerate(ds):

        def write(k, high, low):
            m_ref[n, k, :, :LANES] = high
            m_ref[n, k, :, LANES:] = low

        e_ref[n][...] = whiten_body(x_refs[n], table_ref, mask_ref, scratch.at[n % 2], write)
        outs.append(pltpu.make_async_copy(m_ref.at[n], m_hbm.at[d], out_sem.at[n]))
        outs[-1].start()
    for c in outs:
        c.wait()


def member_shapes(x):
    events, chans, length = x.shape
    bins = length // 2
    m = jax.ShapeDtypeStruct((bins, events, 2 * LANES), BF16)
    return m, (2 * events * chans // LANES * bins, LANES)


ENERGY = jax.ShapeDtypeStruct((8, LANES), F32)


def whiten(xs, table, mask, owners, filled, after):
    ds = sorted(xs)
    count = len(ds)
    m, scratch = member_shapes(xs[ds[0]])
    buffers = [
        pltpu.VMEM(table.shape, table.dtype),
        pltpu.VMEM((count,) + m.shape, m.dtype),
        pltpu.VMEM((2,) + scratch, F32),
        pltpu.SemaphoreType.DMA,
        pltpu.SemaphoreType.DMA((count,)),
    ]
    out = pl.pallas_call(
        functools.partial(whiten_kernel, ds),
        out_shape=[jax.ShapeDtypeStruct((owners,) + m.shape, m.dtype)] + [ENERGY] * count,
        in_specs=[IN_HBM, IN_VMEM] + [IN_VMEM] * (count + len(after)) + [IN_HBM] * len(filled),
        out_specs=[IN_HBM] + [IN_VMEM] * count,
        scratch_shapes=buffers,
        cost_estimate=SHORT,
        input_output_aliases={2 + count + len(after): 0} if filled else {},
        compiler_params=room(buffers),
        name="whiten",
    )(table, mask, *[xs[d] for d in ds], *after, *filled)
    return out[0], dict(zip(ds, out[1:]))


def turn(m):
    half = LANES // 2
    return jnp.concatenate([m[:, half:LANES], -m[:, :half]], axis=1)


def pairs_body(me, new, members, table_ref, cross_ref, copies, emit, ready):
    count, bins, _, _ = members.shape
    slots = count * CAP
    tiles = slots // LANES
    taus = table_ref.shape[0] // 2
    n = len(new) * CAP
    pitch = 2 * bins + PITCH_PAD

    def cross(k, carry):
        both = jnp.concatenate([members[jnp.bitwise_xor(me, b), k] for b in range(count)], axis=0)
        left = jnp.concatenate([members[d, k] for d in new], axis=0)
        high = left[:, :LANES]
        low = left[:, LANES:]
        left = jnp.concatenate([high, turn(high), low, turn(low)], axis=0)
        right = jnp.concatenate([both[:, :LANES], both[:, LANES:]], axis=0)
        if n <= 32:
            out = dot_rows(left, right)
            total = out[: 2 * n, :slots] + (out[: 2 * n, slots:] + out[2 * n :, :slots])
        else:
            out = dot_rows(left[: 2 * n], right)
            total = out[:, :slots] + (out[:, slots:] + dot_rows(left[2 * n :], right[:slots]))
        for q in range(2):
            for t in range(tiles):
                part = total[q * n : (q + 1) * n, t * LANES : (t + 1) * LANES]
                cross_ref[t, pl.ds(q * bins + k, n, stride=pitch), :] = part
        return carry

    step = bins // LOAD_PARTS
    for p in range(LOAD_PARTS):
        copies[p].wait()
        lax.fori_loop(p * step, (p + 1) * step, cross, 0, unroll=32 if n <= 32 else 16)
    table = table_ref[...]

    def lag(i, carry):
        for t in range(tiles):
            pair = cross_ref[t, pl.ds(pl.multiple_of(2 * i * pitch, 8), 2 * pitch), :]
            pair = jnp.concatenate([pair[: 2 * bins], pair[pitch : pitch + 2 * bins]], axis=1)
            high, low = split(pair)
            out = dot(table, high)
            out = out[:taus] + (out[taus:] + dot(table[:taus], low))
            for h in range(2):
                emit(2 * i + h, t, out[:, h * LANES : (h + 1) * LANES])
        return carry

    for start in range(0, n // 2, CAP):
        stop = min(start + CAP, n // 2)
        lax.fori_loop(start, stop, lag, 0, unroll=8)
        ready(2 * stop)


def turn_lines(lines, codes, chan, turned, taus):
    tiles = lines.shape[0] // (CAP * LAGS)
    groups, parts = turned.shape[0], taus // 8
    rows = turned.shape[1] // parts
    for g in range(parts):
        for t in range(tiles):
            pieces = []
            for u in range(7, -1, -1):
                tau = 2 * MAXLAG - 8 * g - u
                if tau >= 0:
                    pieces.append(lines[pl.ds(t * CAP * LAGS + tau, CAP, stride=LAGS), :])
                else:
                    pieces.append(codes[min(-tau, len(codes)) - 1])
            value = jnp.concatenate(pieces, axis=0).T
            for c in range(LANES // rows):
                target = jnp.bitwise_xor(chan, t * (LANES // rows) + c)
                turned[target, g * rows : (g + 1) * rows] = value[c * rows : (c + 1) * rows]


def place(me, d):
    return pl.multiple_of(jnp.bitwise_xor(me, d) * CAP, CAP)


def load_members(m_hbm, count, members, sem):
    step = members.shape[1] // LOAD_PARTS
    copies = []
    for p in range(LOAD_PARTS):
        part = pl.ds(p * step, step)
        source, target = m_hbm.at[pl.ds(0, count), part], members.at[pl.ds(0, count), part]
        copies.append(pltpu.make_async_copy(source, target, sem.at[p]))
        copies[-1].start()
    return copies


def slot_vector(me, tiles, slots):
    lane = lax.broadcasted_iota(jnp.int32, (8, slots), 1) // CAP
    value = jnp.zeros((8, slots), F32)
    for d, tile in tiles.items():
        value = jnp.where(lane == jnp.bitwise_xor(me, d), jnp.concatenate([tile] * (slots // LANES), axis=1), value)
    return value


def as_rows(value, ref):
    for t in range(value.shape[1] // LANES):
        part = jnp.broadcast_to(value[0:1, t * LANES : (t + 1) * LANES], (LANES, LANES))
        ref[t * LANES : (t + 1) * LANES] = part.T


def whiten_and_load(new, count, x_refs, m_hbm, tables, buffers, sems, keep):
    table_hbm, mask_ref = tables
    table_ref, scratch, members = buffers
    load, sem = sems
    table_load = pltpu.make_async_copy(table_hbm, table_ref, load)
    table_load.start()
    copies = load_members(m_hbm, count, members, sem)
    table_load.wait()
    tiles = {}
    for n, d in enumerate(new):

        def write(k, high, low):
            members[d, k, :, :LANES] = high
            members[d, k, :, LANES:] = low

        tiles[d] = whiten_body(x_refs[n], table_ref, mask_ref, scratch.at[n % 2], write)
        keep(d, members.at[d])
    return tiles, copies


def shared_scratch(x, new, table, slots, n):
    m, scratch = member_shapes(x)
    bins = m.shape[0]
    return [
        pltpu.VMEM(table.shape, table.dtype),
        pltpu.VMEM((min(2, len(new)),) + scratch, F32),
        pltpu.VMEM((slots // CAP, bins, CAP, 2 * LANES), BF16),
        pltpu.VMEM((slots // LANES, n * (2 * bins + PITCH_PAD), LANES), F32),
        pltpu.SemaphoreType.DMA,
        pltpu.SemaphoreType.DMA((LOAD_PARTS,)),
        pltpu.SemaphoreType.DMA((24,)),
    ]


def square_kernel(old, new, lines_of, more, me_ref, table_hbm, mask_ref, lag_ref, *refs):
    count = len(new)
    x_refs, refs = refs[:count], refs[count:]
    m_hbm, refs = refs[0], refs[1:]
    given, refs = refs[: len(old)], refs[len(old) :]
    table_ref, scratch, members, cross_ref, load, sem, out_sem, rows_ref = refs[-8:]
    outs = refs[-8 - 1 - count - more : -8]
    me, own = me_ref[0], me_ref[2]
    slots = members.shape[0] * CAP
    done = []

    def keep(d, block):
        if more:
            done.append(pltpu.make_async_copy(block, outs[1 + count].at[d], out_sem.at[8 + len(done)]))
            done[-1].start()

    buffers = (table_ref, scratch, members)
    tables = (table_hbm, mask_ref)
    tiles, copies = whiten_and_load(new, len(old), x_refs, m_hbm, tables, buffers, (load, sem), keep)
    for n, d in enumerate(new):
        outs[1 + n][...] = tiles[d]
    for d, ref in zip(old, given):
        tiles[d] = ref[...]
    codes = code_of(slot_vector(me, tiles, slots))

    def emit(row, t, part):
        rows_ref[row, :, t * LANES : (t + 1) * LANES] = part

    groups, rows = outs[0].shape[:2]
    first = lines_of[0] * CAP // rows

    def ready(stop):
        if stop % rows == 0:
            n = stop // rows - 1
            for c, code in enumerate(codes):
                rows_ref[n * rows, 2 * MAXLAG + 1 + c : 2 * MAXLAG + 2 + c] = code[0:1]
            target = jnp.bitwise_xor(first + n, own)
            part = rows_ref.at[n * rows : (n + 1) * rows]
            done.append(pltpu.make_async_copy(part, outs[0].at[target], out_sem.at[n]))
            done[-1].start()

    pairs_body(me, lines_of, members, lag_ref, cross_ref, copies, emit, ready)
    if first + rows_ref.shape[0] // rows == groups - 1:
        target = jnp.bitwise_xor(groups - 1, own)
        done.append(pltpu.make_async_copy(rows_ref.at[:rows], outs[0].at[target], out_sem.at[groups - 1]))
        done[-1].start()
    for c in done:
        c.wait()


def square(me, xs, table, mask, lags, ms, energy, lines_of, slots, groups, more, after, filled):
    old, new = sorted(energy), sorted(xs)
    taus = lags.shape[0] // 2
    x = xs[new[0]]
    n = len(lines_of) * CAP
    rows = jax.ShapeDtypeStruct((groups, slots // groups, taus, slots), F32)
    members = jax.ShapeDtypeStruct(ms.shape, ms.dtype)
    aliases = {4 + len(new): 1 + len(new)} if more else {}
    if filled:
        aliases[5 + len(new) + len(old) + len(after)] = 0
    buffers = shared_scratch(x, new, table, slots, n) + [pltpu.VMEM((n, taus, slots), F32)]
    return pl.pallas_call(
        functools.partial(square_kernel, old, new, lines_of, more),
        out_shape=[rows] + [ENERGY] * len(new) + [members] * more,
        in_specs=[IN_SMEM, IN_HBM, IN_VMEM, IN_VMEM]
        + [IN_VMEM] * len(new)
        + [IN_HBM]
        + [IN_VMEM] * len(old)
        + [IN_HBM] * (len(after) + len(filled)),
        out_specs=[IN_HBM] + [IN_VMEM] * len(new) + [IN_HBM] * more,
        scratch_shapes=buffers,
        cost_estimate=SHORT,
        input_output_aliases=aliases,
        compiler_params=room(buffers),
        name="square",
    )(me, table, mask, lags, *[xs[d] for d in new], ms, *[energy[d] for d in old], *after, *filled)


def step_kernel(new, final, me_ref, table_hbm, mask_ref, lag_ref, x_ref, m_hbm, *refs):
    lines, turned_ref = refs[-2:]
    table_ref, scratch, members, cross_ref, load, sem, out_sem = refs[-9:-2]
    outs = refs[-9 - (2 if final else 4) : -9]
    me, chan = me_ref[0], me_ref[1]
    slots = members.shape[0] * CAP
    taus = lag_ref.shape[0] // 2
    done = []

    def start(source, target):
        done.append(pltpu.make_async_copy(source, target, out_sem.at[len(done)]))
        done[-1].start()

    def keep(d, block):
        if not final:
            start(block, outs[2].at[d])

    full_turned = turned_ref
    if final:
        kept_turned = refs[0]
        turned_cut = kept_turned.shape[1]
        start(kept_turned, turned_ref.at[:, :turned_cut])
        turned_ref = turned_ref.at[:, turned_cut:]
    buffers = (table_ref, scratch, members)
    tiles, copies = whiten_and_load([new], new, [x_ref], m_hbm, (table_hbm, mask_ref), buffers, (load, sem), keep)
    tile = tiles[new]
    column = jnp.broadcast_to(tile[0:1], (LANES, LANES)).T[:CAP]

    def emit(row, t, part):
        lines[pl.ds((t * CAP + row) * LAGS, LAGS), :] = part[:LAGS]

    pairs_body(me, [new], members, lag_ref, cross_ref, copies, emit, lambda stop: None)
    if final:
        for c in done:
            c.wait()
    else:
        outs[3][...] = tile
    start(lines, outs[0])
    turn_lines(lines, code_of(column), chan, turned_ref, taus)
    start(full_turned, outs[1])
    for c in done[1:] if final else done:
        c.wait()


def step(me, x, table, mask, lags, ms, new, slots, groups, kept, after):
    taus = lags.shape[0] // 2
    final = len(kept) > 0
    parts = taus // 8 * (slots // groups)
    lines = jax.ShapeDtypeStruct((slots // LANES * CAP * LAGS, LANES), F32)
    turned = jax.ShapeDtypeStruct((groups, parts + (kept[0].shape[1] if final else 0), LANES), F32)
    members = jax.ShapeDtypeStruct(ms.shape, ms.dtype)
    buffers = shared_scratch(x, [new], table, slots, CAP)
    buffers += [pltpu.VMEM(lines.shape, F32), pltpu.VMEM(turned.shape, F32)]
    return pl.pallas_call(
        functools.partial(step_kernel, new, final),
        out_shape=[lines, turned] + ([] if final else [members, ENERGY]),
        in_specs=[IN_SMEM, IN_HBM, IN_VMEM, IN_VMEM, IN_VMEM] + [IN_HBM] * (1 + len(kept) + len(after)),
        out_specs=[IN_HBM] * 2 + ([] if final else [IN_HBM, IN_VMEM]),
        scratch_shapes=buffers,
        cost_estimate=LONG if final else SHORT,
        input_output_aliases={} if final else {5: 2},
        compiler_params=room(buffers),
        name="step",
    )(me, table, mask, lags, x, ms, *kept, *after)


def hold_kernel(*refs):
    del refs


def hold(xs, after):
    n = len(xs)
    return pl.pallas_call(
        hold_kernel,
        out_shape=[jax.ShapeDtypeStruct(x.shape, x.dtype) for x in xs],
        in_specs=[IN_HBM] * n + [IN_VMEM] * len(after),
        out_specs=[IN_HBM] * n,
        input_output_aliases={i: i for i in range(n)},
        cost_estimate=SHORT,
        name="hold",
    )(*xs, *after)


def finish_kernel(last, blocks, me_ref, *refs):
    out_hbm, out_ref, lines_sum, rows_ref, sem = refs[-5:]
    me, chan, own = me_ref[0], me_ref[1], me_ref[2]
    lags, rows, slots = out_hbm.shape
    pitch = rows + PITCH_PAD
    tiles = slots // LANES
    groups = slots // rows
    taus = lag_rows()
    parts = taus // 8
    base, turned = refs[:groups], refs[groups : 2 * groups]
    late = [refs[(2 + n) * groups : (3 + n) * groups] for n in range(len(last))]
    scale = [1.0] + [1.0 / F16_SCALE] * (groups - 1)
    lane = lax.broadcasted_iota(jnp.int32, (8, LANES), 1)

    def spread(line, v):
        part = jnp.where(lane < CAP, pltpu.roll(line, LANES - v * CAP, 1), 0.0)
        for shift in (CAP, 2 * CAP, 4 * CAP):
            part = part + pltpu.roll(part, shift, 1)
        return part

    def energy_of(high, low, exponent, e):
        return (high + low) * scale[e] * jnp.exp2(jnp.round(exponent * (64.0 * scale[e])))

    block_of = lax.broadcasted_iota(jnp.int32, (8, slots), 1) // CAP
    every, local = [], []
    for e in range(groups):
        local.append({})
        for n, d in enumerate(last):
            start = (n * parts + parts - 1) * rows
            line = turned[e][start : start + 8]
            local[e][d] = energy_of(spread(line, 6), spread(line, 5), spread(line, 4), e)
        codes = base[e][0, taus - 8 : taus]
        vector = jnp.broadcast_to(energy_of(codes[1:2], codes[2:3], codes[3:4], e), (8, slots))
        for d in last:
            wide = jnp.concatenate([local[e][d]] * tiles, axis=1)
            vector = jnp.where(block_of == jnp.bitwise_xor(me, d), wide, vector)
        every.append(vector)
    norm = lax.rsqrt(sum(every) + 1e-05)
    every = [jnp.sqrt(x) * norm for x in every]
    norms = {d: lax.rsqrt(sum(x[d] for x in local) + 1e-05) for d in last}
    local = [{d: jnp.sqrt(x[d]) * norms[d] for d in last} for x in local]
    for e in range(groups):
        as_rows(every[e] * scale[e], rows_ref.at[e])
    mine = [rows_ref[e, pl.ds(pl.multiple_of(chan * rows, 8), rows), :] for e in range(groups)]
    for n, d in enumerate(last):
        weight = [mine[e] * local[e][d][0:1] for e in range(groups)]
        shift = (jnp.bitwise_xor(me, d) * CAP + LANES - 7 * CAP) % LANES
        for g in range(parts):
            total = 0.0
            for e in range(groups):
                start = (n * parts + g) * rows
                total = total + turned[e][start : start + rows] * weight[e]
            lines_sum[n, g] = pltpu.roll(total, shift, 1)

    def emit(h, from_base):
        d_row = own * blocks + h
        b_row = jnp.bitwise_and(jnp.bitwise_xor(me, d_row), blocks - 1)
        d_late = last[h]

        def one_row(r, carry):
            target = b_row * CAP + r
            slot = jnp.bitwise_xor(me, d_row) * CAP + r
            weight = []
            for e in range(groups):
                row = rows_ref[e, pl.ds(slot, 1), :]
                weight.append(jnp.concatenate([row] * tiles, axis=1) * every[e])
            for g in range(parts):
                stop = min(8, lags - 8 * g)
                value = 0.0
                for e in range(groups):
                    if from_base:
                        part = base[e][h * CAP + r, 8 * g : 8 * g + stop]
                    else:
                        pieces = [late[h][e][pl.ds((t * CAP + r) * LAGS + 8 * g, stop), :] for t in range(tiles)]
                        part = jnp.concatenate(pieces, axis=1)
                    value = value + part * weight[e][:stop]
                for n, d in enumerate(last):
                    if not from_base and d <= d_late:
                        continue
                    line = jnp.broadcast_to(lines_sum[n, g, pl.ds(target, 1), :], (8, LANES))
                    line = pltpu.roll(line, 0, 1, stride=CAP, stride_axis=0)[:stop]
                    line = jnp.concatenate([line] * tiles, axis=1)
                    value = jnp.where(block_of[:stop] == jnp.bitwise_xor(me, d), line, value)
                for t in range(tiles):
                    part = value[:, t * LANES : (t + 1) * LANES]
                    if stop < 8:
                        out_ref[t, 8 * g : 8 * g + stop, pl.ds(target, 1), :] = part.reshape(stop, 1, LANES)
                    else:
                        flat = out_ref.at[t].reshape(lags * pitch, LANES)
                        flat[pl.ds(8 * g * pitch + target, stop, stride=pitch), :] = part
            return carry

        lax.fori_loop(0, CAP, one_row, 0, unroll=2)

    @pl.when(own < groups - 1)
    def _():
        for h in range(blocks):
            emit(h, True)

    @pl.when(own == groups - 1)
    def _():
        for h in range(blocks):
            emit(h, False)

    copies = []
    for t in range(tiles):
        target = out_hbm.at[:, :, t * LANES : (t + 1) * LANES]
        copies.append(pltpu.make_async_copy(out_ref.at[t, :, :rows], target, sem.at[t]))
        copies[-1].start()
    for c in copies:
        c.wait()


def finish(me, base, turned, late, last, blocks):
    rows, taus, slots = base[0].shape
    groups = slots // rows
    lags = 2 * MAXLAG + 1
    out = pl.pallas_call(
        functools.partial(finish_kernel, last, blocks),
        out_shape=jax.ShapeDtypeStruct((lags, rows, slots), F32),
        in_specs=[IN_SMEM] + [IN_VMEM] * ((2 + len(last)) * groups),
        out_specs=IN_HBM,
        scratch_shapes=[
            pltpu.VMEM((slots // LANES, lags, rows + PITCH_PAD, LANES), F32),
            pltpu.VMEM((len(last), taus // 8, rows, LANES), F32),
            pltpu.VMEM((groups, slots, LANES), F32),
            pltpu.SemaphoreType.DMA((slots // LANES,)),
        ],
        cost_estimate=SHORT,
        compiler_params=pltpu.CompilerParams(vmem_limit_bytes=FINISH_LIMIT),
        name="finish",
    )(me, *base, *turned, *[x for rows_of in late for x in rows_of])
    return jnp.transpose(out, (1, 0, 2))


def local(waveforms, family_of, channel_mask):
    owners = lax.axis_size("fam")
    groups = lax.axis_size("chan")
    blocks = owners // groups
    slots = owners * CAP
    rows = blocks * CAP
    chans, length = waveforms.shape[1:]
    fam = lax.axis_index("fam")
    chan = lax.axis_index("chan")
    own = jnp.bitwise_xor(chan, fam // blocks)
    me = jnp.stack([fam, chan, own, fam // blocks]).astype(jnp.int32)

    half_lanes = LANES // 2
    mask = jnp.pad(channel_mask.astype(F32), ((0, 0), (0, half_lanes - chans)))
    mask = jnp.tile(mask, (1, 4))
    table = jnp.asarray(transform_table(length))
    lags = jnp.asarray(lag_table(length))
    taus = lag_rows()

    half = owners // 2
    last = list(range(owners - blocks, owners))
    early = [d for d in range(owners) if d not in last]
    first = list(range(half, half + blocks))
    sends, inbox = {}, {}
    widen = ((0, 0), (0, half_lanes - chans), (0, 0))

    def collect(dests, after):
        sends.update(zip(dests, gather(me, family_of, waveforms, owners, dests, after)))

    def post(d):
        inbox[d] = jnp.pad(lax.ppermute(sends[d], "fam", [(i, i ^ d) for i in range(owners)]), widen)

    def chan_permute(x, e):
        return lax.ppermute(x, "chan", [(i, i ^ e) for i in range(groups)])

    partners = list(range(groups - 1, 0, -1))

    collect(list(range(half + blocks)), [])
    for d in first + list(range(1, half)):
        post(d)
    inbox[0] = jnp.pad(sends[0], widen)
    ms, energy = whiten({0: inbox[0]}, table, mask, owners, [], [])
    ms, got = whiten({1: inbox[1]}, table, mask, owners, [ms], [])
    energy.update(got)
    remaining = list(range(half + blocks, owners))
    collect(remaining, [got[1]] + [inbox[d] for d in range(1, half)])
    for d in remaining:
        post(d)
    after = [sends[remaining[0]]]
    middle = [d for d in early if d not in energy]
    limit = max(1, 16 * 2**20 // (CAP * length * slots * 4))
    per_call = max(n for n in range(blocks, len(early) + 1, blocks) if len(early) % n == 0 and n <= max(limit, blocks))
    filled = []
    for start in range(0, len(early), per_call):
        lines_of = early[start : start + per_call]
        xs = {d: inbox[d] for d in middle}
        more = int(start == 0)
        result = square(me, xs, table, mask, lags, ms, energy, lines_of, slots, groups, more, after, filled)
        filled = [result[0]]
        after = [result[1]]
        if more:
            ms = result[-1]

    def narrow(x):
        return (x * F16_SCALE).astype(jnp.float16)

    early_rows = filled[0].reshape(groups, rows * taus, slots)
    sent = {e: chan_permute(narrow(early_rows[e]), e) for e in partners}

    def to_owner(x, e):
        moves = []
        for f in range(owners):
            owner = (f // blocks) ^ (groups - 1)
            moves.append(((owner ^ e) * owners + f, owner * owners + f))
        return lax.ppermute(x, ("chan", "fam"), moves)

    kept, late = [], []
    for n, d in enumerate(last):
        result = step(me, inbox[d], table, mask, lags, ms, d, slots, groups, kept, after)
        kept, after = [result[1]], []
        small = narrow(result[0])
        late.append([result[0]] + [to_owner(small, e) for e in range(1, groups)])
        if n < len(last) - 1:
            ms = result[2]
    there = [sent[e] for e in partners] + [x for rows_of in late[:-1] for x in rows_of[1:]]
    (turned,) = hold(kept, [sum(x[:8, :LANES].astype(F32) for x in there)])

    base_parts, turned_parts = [filled[0][0]], [turned[0]]
    for e in range(1, groups):
        base_parts.append(sent[e].astype(F32).reshape(rows, taus, slots))
        turned_parts.append(chan_permute(narrow(turned[e]), e).astype(F32))
    late = [[x.astype(F32) for x in rows_of] for rows_of in late]
    return finish(me, base_parts, turned_parts, late, last, blocks)[None]


def solution(mesh):
    in_specs = (P("fam", "chan", None), P("fam"), P("fam", "chan"))
    out_specs = P("fam", "chan", None, None)
    return jax.shard_map(local, mesh=mesh, in_specs=in_specs, out_specs=out_specs, check_vma=False)
```
